256 devices in a mesh: fsdp: 32 (over x, y, core), expert: 8 (over z).
Axes of the slice: x: 4, y: 4, z: 8, core: 2. Of those that a mesh axis runs over, the one named last changes fastest.
Arguments:
- grads: bfloat16 [8, 7168, 2048], P(None, ('fsdp', 'expert')), may hold values from -6 to 6
- momentum: float32 [8, 7168, 2048], P(None, ('fsdp', 'expert')), may hold values from -6 to 6
- max_logits: float32 [256, 64], P(('fsdp', 'expert')), may hold values from 4 to 500
- q_weight: bfloat16 [1536, 12288], P('fsdp', 'expert'), may hold values from -6 to 6
- k_weight: bfloat16 [512, 8192], P('fsdp', 'expert'), may hold values from -6 to 6
Outputs:
- new_momentum: float32 [8, 7168, 2048], P(None, ('fsdp', 'expert'))
- step: bfloat16 [8, 7168, 2048], P(None, ('fsdp', 'expert'))
- q_clipped: bfloat16 [1536, 12288], P('fsdp', 'expert')
- k_clipped: bfloat16 [512, 8192], P('fsdp', 'expert')
The draws below stay inside these ranges and needn't reach their ends.
All inputs are finite; a program needn't handle non-finite values. Where the reference program divides by a largest or mean magnitude, that divisor is 1e-20 or more.
Results may differ from the reference program's by a relative error of at most 0.012.
Values may be sent and summed in bfloat16 or wider, within the bound.
No kernel may reach another device: no remote copies, remote signals or barrier semaphores. Data moves between devices by JAX's collectives and lax.ppermute only.
A program may use at most 128 MiB of HBM per device.

```python
import jax
import jax.numpy as jnp
from jax import lax

D = 7168
FF = 2048
HEADS = 64
NOPE = 128
ROPE = 64
QLORA = 1536
KVLORA = 512
MATS = 8
ROWS = 256
N_FSDP = 32


def draw_max_logits(key, part):
    key = jax.random.fold_in(key, 7)
    head_key, ratio_key, place_key, row_key = jax.random.split(key, 4)
    head_level = jnp.exp(jax.random.uniform(head_key, (HEADS,), jnp.float32, jnp.log(20.0), jnp.log(500.0)))
    ratio = jnp.exp(jax.random.uniform(ratio_key, (HEADS,), jnp.float32, jnp.log(0.2), jnp.log(0.5)))
    peak_row = jax.random.randint(place_key, (HEADS,), 0, ROWS)
    wobble = jax.random.uniform(row_key, (ROWS, HEADS), jnp.float32, 0.7, 1.0)
    is_peak = jnp.arange(ROWS, dtype=jnp.int32)[:, None] == peak_row[None, :]
    others = head_level[None, :] * ratio[None, :] * wobble
    values = jnp.where(is_peak, head_level[None, :], others)
    return jnp.clip(values, 4.0, 500.0)


def block_levels(own_key, shape, shards, least, largest):
    level, own = 1.0, jax.random.fold_in(own_key, 6)
    for dim, blocks in shards:
        draws = jnp.exp(jax.random.uniform(jax.random.fold_in(own, dim), (blocks,), jnp.float32, least / len(shards), largest / len(shards)))
        level = level * jnp.repeat(draws, shape[dim] // blocks).reshape([-1 if axis == dim else 1 for axis in range(len(shape))])
    return level


def noise(rng, dims, width, limit, shards=(), kind=jnp.bfloat16):
    result = jax.random.normal(rng, dims, jnp.float32) * width
    if len(shards) > 0:
        result = block_levels(rng, dims, shards, -0.22, 0.18) * result
    return jnp.clip(result, min=-limit, max=limit).astype(kind)


def setup_inputs(seed: int = 0) -> dict:
    arg_keys = jax.random.split(jax.random.key(seed), 6)
    grads = noise(arg_keys[0], (MATS, D, FF), 1.0, 6.0, ((1, 256),))
    momentum = noise(arg_keys[1], (MATS, D, FF), 1.0, 6.0, ((1, 256),), jnp.float32)
    max_logits = draw_max_logits(jax.random.fold_in(arg_keys[5], 71), 0)
    q_weight = noise(arg_keys[3], (QLORA, HEADS * (NOPE + ROPE)), 1.0, 6.0, ((0, 32), (1, 8)))
    k_weight = noise(arg_keys[4], (KVLORA, HEADS * NOPE), 1.0, 6.0, ((0, 32), (1, 8)))
    return dict(grads=grads, momentum=momentum, max_logits=max_logits, q_weight=q_weight, k_weight=k_weight)


decay_rate = 0.9
linear_coef = 3.4445
cubic_coef = -4.775
quintic_coef = 2.0315
clip_limit = 100.0
rms_match = 0.2

def orthogonal(direction):
    blocks = direction.reshape(N_FSDP, D // N_FSDP, FF).astype(jnp.float32)

    def add_block(total, block):
        partial_term = jnp.dot(block.T, block, precision=lax.Precision.HIGHEST)
        rounded = lax.optimization_barrier(partial_term.astype(jnp.bfloat16))
        return (total + rounded.astype(jnp.float32), None)
    gram, _ = lax.scan(add_block, jnp.zeros((FF, FF), jnp.float32), blocks)
    bound = jnp.max(lax.optimization_barrier(jnp.sum(jnp.abs(gram), axis=1)))
    gram_scaled = (gram / bound).astype(jnp.bfloat16).astype(jnp.float32)
    start = direction.astype(jnp.float32)
    first = jnp.dot(start, gram_scaled, precision=lax.Precision.HIGHEST)
    first_rounded = first.astype(jnp.bfloat16).astype(jnp.float32)
    second = jnp.dot(first_rounded, gram_scaled, precision=lax.Precision.HIGHEST)
    ortho = (linear_coef * start + cubic_coef * first + quintic_coef * second) / jnp.sqrt(bound)
    return (rms_match * jnp.sqrt(jnp.float32(max(D, FF))) * ortho).astype(jnp.bfloat16)

def reference(grads, momentum, max_logits, q_weight, k_weight):
    new_momentum = decay_rate * momentum + grads.astype(jnp.float32)
    direction = (grads.astype(jnp.float32) + decay_rate * new_momentum).astype(jnp.bfloat16)
    step = lax.map(orthogonal, direction)
    peak = lax.optimization_barrier(jnp.max(max_logits, axis=0))
    gamma = jnp.minimum(1.0, clip_limit / peak)
    root = jnp.sqrt(gamma)
    q_factor = jnp.concatenate([jnp.broadcast_to(root[:, None], (HEADS, NOPE)), jnp.broadcast_to(gamma[:, None], (HEADS, ROPE))], axis=1).reshape(-1)
    q_clipped = (q_weight.astype(jnp.float32) * q_factor[None, :]).astype(jnp.bfloat16)
    k_factor = jnp.broadcast_to(root[:, None], (HEADS, NOPE)).reshape(-1)
    k_clipped = (k_weight.astype(jnp.float32) * k_factor[None, :]).astype(jnp.bfloat16)
    return (new_momentum, step, q_clipped, k_clipped)
```

```python
import math

import jax
import jax.numpy as jnp
from jax import lax
from jax.experimental import pallas as pl
from jax.experimental.pallas import tpu as pltpu
from jax.sharding import Mesh, PartitionSpec as P

D = 7168
FF = 2048
NOPE = 128
ROPE = 64

decay_rate = 0.9
linear_coef = 3.4445
cubic_coef = -4.775
quintic_coef = 2.0315
clip_limit = 100.0
rms_match = 0.2

NX, NY, NC, NZ = 4, 4, 2, 8
CHIPS = NX * NY
BLK = 128
NB = FF // BLK
HALF = FF // 2
BAND = (NB // 2 + 1) * BLK
ROWS = HALF // CHIPS
PADROWS = 32
KROWS = NZ * PADROWS

VMEM = pltpu.CompilerParams(vmem_limit_bytes=50 * 1024 * 1024)
MASS = pl.BlockSpec(memory_space=pltpu.VMEM)


def gram_kernel(core_ref, mine_ref, other_ref, out_ref, rows_ref):
    core = core_ref[0]
    for half in range(2):
        source = pl.ds(pl.multiple_of(((core + half) % 2) * HALF, HALF), HALF)
        here = pl.ds(half * HALF, HALF)
        rows_ref[0:KROWS, here] = mine_ref[:, source]
        rows_ref[KROWS : 2 * KROWS, here] = other_ref[:, source]
    for pair in range(NB // 4):
        left = rows_ref[:, pl.ds(pair * 2 * BLK, 2 * BLK)]
        right = rows_ref[:, pl.ds(pair * 2 * BLK, BAND + BLK)]
        product = lax.dot_general(
            left, right, (((0,), (0,)), ((), ())), preferred_element_type=jnp.float32
        ).astype(jnp.bfloat16)
        for sub in range(2):
            for part in range(BLK // ROWS):
                row = sub * BLK + part * ROWS
                chunk = (pair * 2 + sub) * (BLK // ROWS) + part
                out_ref[chunk] = product[row : row + ROWS, sub * BLK : sub * BLK + BAND]


def gram_band(core, mine, other):
    return pl.pallas_call(
        gram_kernel,
        out_shape=jax.ShapeDtypeStruct((CHIPS, ROWS, BAND), jnp.bfloat16),
        in_specs=[pl.BlockSpec(memory_space=pltpu.SMEM), MASS, MASS],
        out_specs=MASS,
        scratch_shapes=[pltpu.VMEM((2 * KROWS, FF), jnp.bfloat16)],
        compiler_params=VMEM,
        name="gram_band",
    )(core, mine, other)


def step_kernel(place_ref, mine_ref, *refs):
    pieces = refs[:16]
    out_ref, band_ref, gram_ref, x_ref, first_ref, round_ref = refs[16:]
    x, y, core = place_ref[0], place_ref[1], place_ref[2]
    for half in range(2):
        source = pl.ds(pl.multiple_of(((core + half) % 2) * HALF, HALF), HALF)
        x_ref[:, pl.ds(half * HALF, HALF)] = mine_ref[:, source]
    for side in range(2):
        for kind in range(2):
            for outer in range(4):
                piece = pieces[side * 8 + kind * 4 + outer]
                for inner in range(4):
                    dx, dy = (inner, outer) if kind == 0 else (outer, inner)
                    chip = ((x + (4 - dx)) % 4) * 4 + (y + (4 - dy)) % 4
                    row = pl.multiple_of(side * HALF + chip * ROWS + kind * (ROWS // 2), ROWS // 2)
                    band_ref[pl.ds(row, ROWS // 2), :] = piece[inner]
    for i in range(NB):
        block = band_ref[pl.ds(i * BLK, BLK), :]
        turned = block[:, BLK : BAND - BLK].T
        for d in range(NB // 2 + 1):
            j = (i + d) % NB
            gram_ref[pl.ds(i * BLK, BLK), pl.ds(j * BLK, BLK)] = block[:, d * BLK : (d + 1) * BLK]
            if 1 <= d < NB // 2:
                gram_ref[pl.ds(j * BLK, BLK), pl.ds(i * BLK, BLK)] = turned[(d - 1) * BLK : d * BLK]

    def add_rows(k, total):
        part = jnp.abs(gram_ref[pl.ds(pl.multiple_of(k * 64, 64), 64), :].astype(jnp.float32))
        return total + jnp.sum(part.reshape(8, 8, FF), axis=0)

    sums = lax.fori_loop(0, FF // 64, add_rows, jnp.zeros((8, FF), jnp.float32))
    bound = jnp.max(jnp.sum(sums, axis=0, keepdims=True))
    bound = jnp.full((1, 1), bound, jnp.float32)
    inverse = 1.0 / bound
    scale = rms_match * math.sqrt(max(D, FF)) / jnp.sqrt(bound)
    WIDE = 512
    for n in range(FF // WIDE):
        columns = pl.ds(n * WIDE, WIDE)
        first = jnp.dot(x_ref[...], gram_ref[:, columns], preferred_element_type=jnp.float32) * inverse
        first_ref[:, columns] = linear_coef * x_ref[:, columns].astype(jnp.float32) + cubic_coef * first
        round_ref[:, columns] = first.astype(jnp.bfloat16)
    for n in range(FF // WIDE):
        columns = pl.ds(n * WIDE, WIDE)
        second = jnp.dot(round_ref[...], gram_ref[:, columns], preferred_element_type=jnp.float32) * inverse
        step = scale * (first_ref[:, columns] + quintic_coef * second)
        target = (n * WIDE + core * HALF) % FF
        out_ref[:, pl.ds(pl.multiple_of(target, WIDE), WIDE)] = step.astype(jnp.bfloat16)


def finish(place, mine, pieces):
    return pl.pallas_call(
        step_kernel,
        out_shape=jax.ShapeDtypeStruct((KROWS, FF), jnp.bfloat16),
        in_specs=[pl.BlockSpec(memory_space=pltpu.SMEM)] + [MASS] * 17,
        out_specs=MASS,
        scratch_shapes=[
            pltpu.VMEM((FF, BAND), jnp.bfloat16),
            pltpu.VMEM((FF, FF), jnp.bfloat16),
            pltpu.VMEM((KROWS, FF), jnp.bfloat16),
            pltpu.VMEM((KROWS, FF), jnp.float32),
            pltpu.VMEM((KROWS, FF), jnp.bfloat16),
        ],
        compiler_params=VMEM,
        name="finish",
    )(place, mine, *pieces)


def shift(value, axis, by, size):
    return lax.ppermute(value, axis, [(i, (i + by) % size) for i in range(size)])


def swap_cores(value):
    return lax.ppermute(value, "c", [(0, 1), (1, 0)])


def spread(value, axis):
    return [value] + [shift(value, axis, d, 4) for d in range(1, 4)]


def body(grads, momentum, max_logits, q_weight, k_weight):
    x, y, core = lax.axis_index("x"), lax.axis_index("y"), lax.axis_index("c")
    place = jnp.stack([x, y, core]).astype(jnp.int32)
    new_momentum = decay_rate * momentum + grads.astype(jnp.float32)
    direction = (grads.astype(jnp.float32) + decay_rate * new_momentum).astype(jnp.bfloat16)
    direction = jnp.pad(direction, ((0, 0), (0, PADROWS - direction.shape[1]), (0, 0)))
    owned = lax.all_to_all(direction, "z", split_axis=0, concat_axis=0, tiled=True)
    owned = owned.reshape(KROWS, FF)
    band = gram_band(place[2:], owned, swap_cores(owned))
    band = lax.all_to_all(band, ("x", "y"), split_axis=0, concat_axis=0, tiled=True)
    band = jnp.sum(band.astype(jnp.float32), axis=0).astype(jnp.bfloat16)
    a, b = band[: ROWS // 2], band[ROWS // 2 :]
    a = jnp.stack(spread(a, "x"))
    b = jnp.stack(spread(b, "y"))
    own = spread(a, "y") + spread(b, "x")
    other = [swap_cores(piece) for piece in own]
    step = finish(place, owned, own + other).reshape(NZ, PADROWS, FF)
    step = lax.all_to_all(step, "z", split_axis=0, concat_axis=0, tiled=True)
    step = step[:, : grads.shape[1]]

    logits = lax.all_gather(jnp.pad(max_logits, ((0, 7), (0, 64))), ("x", "y", "c", "z"))
    peak = jnp.max(logits[:, 0, :64], axis=0)
    gamma = jnp.minimum(1.0, clip_limit / peak)
    root = jnp.sqrt(gamma)
    local_heads = k_weight.shape[1] // NOPE
    first_head = lax.axis_index("z") * local_heads
    gamma_mine = lax.dynamic_slice_in_dim(gamma, first_head, local_heads)
    root_mine = lax.dynamic_slice_in_dim(root, first_head, local_heads)
    q_factor = jnp.concatenate(
        [
            jnp.broadcast_to(root_mine[:, None], (local_heads, NOPE)),
            jnp.broadcast_to(gamma_mine[:, None], (local_heads, ROPE)),
        ],
        axis=1,
    )
    q_view = q_weight.reshape(q_weight.shape[0], local_heads, NOPE + ROPE).astype(jnp.float32)
    q_clipped = (q_view * q_factor[None]).astype(jnp.bfloat16).reshape(q_weight.shape)
    k_view = k_weight.reshape(k_weight.shape[0], local_heads, NOPE).astype(jnp.float32)
    k_clipped = (k_view * root_mine[None, :, None]).astype(jnp.bfloat16).reshape(k_weight.shape)
    return (new_momentum, step, q_clipped, k_clipped)


def solution(mesh):
    split = Mesh(mesh.devices.reshape(NX, NY, NC, NZ), ("x", "y", "c", "z"))
    rows = P(None, ("x", "y", "c", "z"), None)
    heads = P(("x", "y", "c"), "z")
    return jax.shard_map(
        body,
        mesh=split,
        in_specs=(rows, rows, P(("x", "y", "c", "z"), None), heads, heads),
        out_specs=(rows, rows, heads, heads),
        check_vma=False,
    )
```

```python
import math

import jax
import jax.numpy as jnp
from jax import lax
from jax.experimental import pallas as pl
from jax.experimental.pallas import tpu as pltpu
from jax.sharding import Mesh, PartitionSpec as P

D = 7168
FF = 2048
NOPE = 128
ROPE = 64

decay_rate = 0.9
linear_coef = 3.4445
cubic_coef = -4.775
quintic_coef = 2.0315
clip_limit = 100.0
rms_match = 0.2

NX, NY, NC, NZ = 4, 4, 2, 8
BLK = 128
NB = FF // BLK
HALF = FF // 2
BAND = (NB // 2 + 1) * BLK
PADROWS = 32
KROWS = NZ * PADROWS
CUT = 512
TAIL = 384
PACKED = FF + (FF // CUT) * TAIL
SHARE = BLK // 4

MASS = pl.BlockSpec(memory_space=pltpu.VMEM)
SCALARS = pl.BlockSpec(memory_space=pltpu.SMEM)


def room(mib):
    return pltpu.CompilerParams(vmem_limit_bytes=mib * 1024 * 1024)


def low_rows(value):
    return lax.broadcasted_iota(jnp.int32, value.shape, 1) < 4


def pack(tiles):
    t0, t1, t2, t3 = tiles
    e2, e3 = t2[:, :, TAIL:], t3[:, :, TAIL:]
    moved = jnp.concatenate([pltpu.roll(e2, 4, 1), e2, pltpu.roll(e3, 4, 1)], axis=2)
    last = t3[:, :, :TAIL]
    last = jnp.where(low_rows(last), last, moved)
    head = jnp.concatenate([t0, t1], axis=1)
    tail = jnp.concatenate([t2[:, :, :TAIL], last], axis=1)
    return head.astype(jnp.bfloat16), tail.astype(jnp.bfloat16)


def unpack(head, tail):
    head, tail = head.astype(jnp.float32), tail.astype(jnp.float32)
    t2, last = tail[:, :8], tail[:, 8:]
    m0, m1, m2 = last[:, :, :BLK], last[:, :, BLK : 2 * BLK], last[:, :, 2 * BLK :]
    e2 = jnp.where(low_rows(m0), pltpu.roll(m0, 4, 1), m1)
    e3 = pltpu.roll(m2, 4, 1)
    t2 = jnp.concatenate([t2, e2], axis=2)
    t3 = jnp.concatenate([last, e3], axis=2)
    t3 = jnp.where(low_rows(t3), t3, 0.0)
    return head[:, :8], head[:, 8:], t2, t3


def head_columns(n):
    return pl.ds(pl.multiple_of(n * CUT, CUT), CUT)


def tail_columns(n):
    return pl.ds(pl.multiple_of(FF + n * TAIL, BLK), TAIL)


def direction_kernel(grads_ref, momentum_ref, new_ref, out_ref):
    n = pl.program_id(0)
    grads = grads_ref[...].astype(jnp.float32)
    new = decay_rate * momentum_ref[...] + grads
    new_ref[...] = new
    direction = grads + decay_rate * new
    rows, mats, columns = direction.shape
    direction = jnp.concatenate([direction, jnp.zeros((PADROWS - rows, mats, columns), jnp.float32)], axis=0)
    head, tail = pack([jnp.swapaxes(direction[8 * t : 8 * t + 8], 0, 1) for t in range(4)])
    out_ref[:, :, head_columns(n)] = head
    out_ref[:, :, tail_columns(n)] = tail


def find_direction(grads, momentum):
    rows, mats = grads.shape[:2]
    cut = pl.BlockSpec((rows, mats, CUT), lambda n: (0, 0, n))
    return pl.pallas_call(
        direction_kernel,
        grid=(FF // CUT,),
        out_shape=(
            jax.ShapeDtypeStruct(grads.shape, jnp.float32),
            jax.ShapeDtypeStruct((mats, 16, PACKED), jnp.bfloat16),
        ),
        in_specs=[cut, cut],
        out_specs=(cut, pl.BlockSpec((mats, 16, PACKED), lambda n: (0, 0, 0))),
        compiler_params=room(24),
        name="find_direction",
    )(grads, momentum)


def spread_kernel(packed_ref, out_ref):
    n = pl.program_id(0)
    tiles = unpack(packed_ref[:, :, head_columns(n)], packed_ref[:, :, tail_columns(n)])
    rows = jnp.concatenate([jnp.swapaxes(t, 0, 1) for t in tiles], axis=0)
    out_ref[...] = rows[: out_ref.shape[0]].astype(jnp.bfloat16)


def spread_step(packed, rows):
    return pl.pallas_call(
        spread_kernel,
        grid=(FF // CUT,),
        out_shape=jax.ShapeDtypeStruct((rows, NZ, FF), jnp.bfloat16),
        in_specs=[pl.BlockSpec((NZ, 16, PACKED), lambda n: (0, 0, 0))],
        out_specs=pl.BlockSpec((rows, NZ, CUT), lambda n: (0, 0, n)),
        compiler_params=room(16),
        name="spread_step",
    )(packed)


def gram_kernel(place_ref, mine_ref, other_ref, *refs):
    shares, (x_ref, rows_ref, band_ref) = refs[:8], refs[8:]
    x, y, core = place_ref[0], place_ref[1], place_ref[2]
    for n in range(FF // CUT):
        source = (n + 2 * core) % 4
        columns = pl.ds(n * CUT, CUT)
        for half, packed in enumerate((mine_ref, other_ref)):
            tiles = unpack(packed[:, :, head_columns(source)], packed[:, :, tail_columns(source)])
            rows = jnp.concatenate(tiles, axis=1).reshape(KROWS, CUT).astype(jnp.bfloat16)
            rows_ref[pl.ds(half * KROWS, KROWS), columns] = rows
            if half == 0:
                x_ref[:, columns] = rows
    for pair in range(NB // 4):
        left = rows_ref[:, pl.ds(pair * 2 * BLK, 2 * BLK)]
        right = rows_ref[:, pl.ds(pair * 2 * BLK, BAND + BLK)]
        product = lax.dot_general(
            left, right, (((0,), (0,)), ((), ())), preferred_element_type=jnp.float32
        ).astype(jnp.bfloat16)
        for sub in range(2):
            band_ref[pl.ds((pair * 2 + sub) * BLK, BLK), :] = product[
                sub * BLK : (sub + 1) * BLK, sub * BLK : sub * BLK + BAND
            ]
    for d in range(4):
        shares[d][...] = band_ref[pl.ds(pl.multiple_of(((x + d) % 4) * BLK, BLK), BLK), :]
        shares[4 + d][...] = band_ref[pl.ds(pl.multiple_of((4 + (y + d) % 4) * BLK, BLK), BLK), :]


def gram_band(place, mine, other):
    return pl.pallas_call(
        gram_kernel,
        out_shape=[jax.ShapeDtypeStruct((BLK, BAND), jnp.bfloat16)] * 8
        + [jax.ShapeDtypeStruct((KROWS, FF), jnp.bfloat16)],
        in_specs=[SCALARS, MASS, MASS],
        out_specs=[MASS] * 9,
        scratch_shapes=[
            pltpu.VMEM((2 * KROWS, FF), jnp.bfloat16),
            pltpu.VMEM((HALF, BAND), jnp.bfloat16),
        ],
        compiler_params=room(28),
        name="gram_band",
    )(place, mine, other)


def partial_kernel(place_ref, *refs):
    parts, outs = refs[:8], refs[8:]
    for kind in range(2):
        here = place_ref[1 - kind]
        for d in range(4):
            rows = pl.ds(pl.multiple_of(((here + d) % 4) * SHARE, SHARE), SHARE)
            total = sum(part[rows, :].astype(jnp.float32) for part in parts[4 * kind : 4 * kind + 4])
            outs[4 * kind + d][...] = total.astype(jnp.bfloat16)


def partial_sums(place, parts):
    return pl.pallas_call(
        partial_kernel,
        out_shape=[jax.ShapeDtypeStruct((SHARE, BAND), jnp.bfloat16)] * 8,
        in_specs=[SCALARS] + [MASS] * 8,
        out_specs=[MASS] * 8,
        compiler_params=room(16),
        name="partial_sums",
    )(place, *parts)


def total_kernel(*refs):
    parts, outs = refs[:8], refs[8:]
    for kind in range(2):
        total = sum(part[...].astype(jnp.float32) for part in parts[4 * kind : 4 * kind + 4])
        outs[kind][...] = total.astype(jnp.bfloat16)


def total_sums(parts):
    return pl.pallas_call(
        total_kernel,
        out_shape=[jax.ShapeDtypeStruct((SHARE, BAND), jnp.bfloat16)] * 2,
        in_specs=[MASS] * 8,
        out_specs=[MASS] * 2,
        compiler_params=room(16),
        name="total_sums",
    )(*parts)


def step_kernel(place_ref, x_ref, *refs):
    pieces = refs[:16]
    out_ref, band_ref, gram_ref, first_ref, round_ref = refs[16:]
    x, y, core = place_ref[0], place_ref[1], place_ref[2]
    for side in range(2):
        for kind in range(2):
            for outer in range(4):
                piece = pieces[side * 8 + kind * 4 + outer]
                for inner in range(4):
                    dx, dy = (inner, outer) if kind == 0 else (outer, inner)
                    sx, sy = (x + (4 - dx)) % 4, (y + (4 - dy)) % 4
                    share = sx * 4 + sy if kind == 0 else 16 + sy * 4 + sx
                    row = pl.multiple_of(side * HALF + share * SHARE, SHARE)
                    band_ref[pl.ds(row, SHARE), :] = piece[inner]
    for i in range(NB):
        block = band_ref[pl.ds(i * BLK, BLK), :]
        turned = block[:, BLK : BAND - BLK].T
        for d in range(NB // 2 + 1):
            j = (i + d) % NB
            gram_ref[pl.ds(i * BLK, BLK), pl.ds(j * BLK, BLK)] = block[:, d * BLK : (d + 1) * BLK]
            if 1 <= d < NB // 2:
                gram_ref[pl.ds(j * BLK, BLK), pl.ds(i * BLK, BLK)] = turned[(d - 1) * BLK : d * BLK]

    def add_rows(k, total):
        part = jnp.abs(gram_ref[pl.ds(pl.multiple_of(k * 64, 64), 64), :].astype(jnp.float32))
        return total + jnp.sum(part.reshape(8, 8, FF), axis=0)

    sums = lax.fori_loop(0, FF // 64, add_rows, jnp.zeros((8, FF), jnp.float32))
    bound = jnp.max(jnp.sum(sums, axis=0, keepdims=True))
    bound = jnp.full((1, 1), bound, jnp.float32)
    inverse = 1.0 / bound
    scale = rms_match * math.sqrt(max(D, FF)) / jnp.sqrt(bound)
    for n in range(FF // CUT):
        columns = pl.ds(n * CUT, CUT)
        first = jnp.dot(x_ref[...], gram_ref[:, columns], preferred_element_type=jnp.float32) * inverse
        first_ref[:, columns] = linear_coef * x_ref[:, columns].astype(jnp.float32) + cubic_coef * first
        round_ref[:, columns] = first.astype(jnp.bfloat16)
    for n in range(FF // CUT):
        columns = pl.ds(n * CUT, CUT)
        second = jnp.dot(round_ref[...], gram_ref[:, columns], preferred_element_type=jnp.float32) * inverse
        step = scale * (first_ref[:, columns] + quintic_coef * second)
        step = step.reshape(NZ, PADROWS, CUT)
        head, tail = pack([step[:, 8 * t : 8 * t + 8] for t in range(4)])
        target = (n + 2 * core) % 4
        out_ref[:, :, head_columns(target)] = head
        out_ref[:, :, tail_columns(target)] = tail


def finish(place, mine, pieces):
    return pl.pallas_call(
        step_kernel,
        out_shape=jax.ShapeDtypeStruct((NZ, 16, PACKED), jnp.bfloat16),
        in_specs=[SCALARS] + [MASS] * 17,
        out_specs=MASS,
        scratch_shapes=[
            pltpu.VMEM((FF, BAND), jnp.bfloat16),
            pltpu.VMEM((FF, FF), jnp.bfloat16),
            pltpu.VMEM((KROWS, FF), jnp.float32),
            pltpu.VMEM((KROWS, FF), jnp.bfloat16),
        ],
        compiler_params=room(40),
        name="finish",
    )(place, mine, *pieces)


def shift(value, axis, by, size):
    return lax.ppermute(value, axis, [(i, (i + by) % size) for i in range(size)])


def swap_cores(value):
    return lax.ppermute(value, "c", [(0, 1), (1, 0)])


def spread(value, axis):
    return [value] + [shift(value, axis, d, 4) for d in range(1, 4)]


def largest(value):
    for axis, size in (("c", NC), ("x", NX), ("y", NY), ("z", NZ)):
        by = 1
        while by < size:
            value = jnp.maximum(value, shift(value, axis, by, size))
            by *= 2
    return value


def body(grads, momentum, max_logits, q_weight, k_weight):
    x, y, core = lax.axis_index("x"), lax.axis_index("y"), lax.axis_index("c")
    place = jnp.stack([x, y, core]).astype(jnp.int32)
    rows = grads.shape[1]
    new_momentum, direction = find_direction(jnp.swapaxes(grads, 0, 1), jnp.swapaxes(momentum, 0, 1))
    new_momentum = jnp.swapaxes(new_momentum, 0, 1)
    owned = lax.all_to_all(direction, "z", split_axis=0, concat_axis=0, tiled=True)
    *shares, mine = gram_band(place, owned, swap_cores(owned))
    parts = [shares[0]] + [shift(shares[d], "x", d, 4) for d in range(1, 4)]
    parts += [shares[4]] + [shift(shares[4 + d], "y", d, 4) for d in range(1, 4)]
    shares = partial_sums(place, parts)
    parts = [shares[0]] + [shift(shares[d], "y", d, 4) for d in range(1, 4)]
    parts += [shares[4]] + [shift(shares[4 + d], "x", d, 4) for d in range(1, 4)]
    a, b = total_sums(parts)
    a = jnp.stack(spread(a, "x"))
    b = jnp.stack(spread(b, "y"))
    own = spread(a, "y") + spread(b, "x")
    other = [swap_cores(piece) for piece in own]
    step = finish(place, mine, own + other)
    step = lax.all_to_all(step, "z", split_axis=0, concat_axis=0, tiled=True)
    step = jnp.swapaxes(spread_step(step, rows), 0, 1)

    peak = largest(max_logits)[0]
    gamma = jnp.minimum(1.0, clip_limit / peak)
    root = jnp.sqrt(gamma)
    local_heads = k_weight.shape[1] // NOPE
    first_head = lax.axis_index("z") * local_heads
    gamma_mine = lax.dynamic_slice_in_dim(gamma, first_head, local_heads)
    root_mine = lax.dynamic_slice_in_dim(root, first_head, local_heads)
    q_factor = jnp.concatenate(
        [
            jnp.broadcast_to(root_mine[:, None], (local_heads, NOPE)),
            jnp.broadcast_to(gamma_mine[:, None], (local_heads, ROPE)),
        ],
        axis=1,
    )
    q_view = q_weight.reshape(q_weight.shape[0], local_heads, NOPE + ROPE).astype(jnp.float32)
    q_clipped = (q_view * q_factor[None]).astype(jnp.bfloat16).reshape(q_weight.shape)
    k_view = k_weight.reshape(k_weight.shape[0], local_heads, NOPE).astype(jnp.float32)
    k_clipped = (k_view * root_mine[None, :, None]).astype(jnp.bfloat16).reshape(k_weight.shape)
    return (new_momentum, step, q_clipped, k_clipped)


def solution(mesh):
    split = Mesh(mesh.devices.reshape(NX, NY, NC, NZ), ("x", "y", "c", "z"))
    rows = P(None, ("x", "y", "c", "z"), None)
    heads = P(("x", "y", "c"), "z")
    return jax.shard_map(
        body,
        mesh=split,
        in_specs=(rows, rows, P(("x", "y", "c", "z"), None), heads, heads),
        out_specs=(rows, rows, heads, heads),
        check_vma=False,
    )
```

```python
import math

import jax
import jax.numpy as jnp
from jax import lax
from jax.experimental import pallas as pl
from jax.experimental.pallas import tpu as pltpu
from jax.sharding import Mesh, PartitionSpec as P

D = 7168
FF = 2048
NOPE = 128
ROPE = 64

decay_rate = 0.9
linear_coef = 3.4445
cubic_coef = -4.775
quintic_coef = 2.0315
clip_limit = 100.0
rms_match = 0.2

NX, NY, NC, NZ = 4, 4, 2, 8
BLK = 128
NB = FF // BLK
HALF = FF // 2
BAND = (NB // 2 + 1) * BLK
PADROWS = 32
KROWS = NZ * PADROWS
CUT = 512
TAIL = 384
PACKED = FF + (FF // CUT) * TAIL
HOLD = BLK // 2

MASS = pl.BlockSpec(memory_space=pltpu.VMEM)
SCALARS = pl.BlockSpec(memory_space=pltpu.SMEM)


def room(mib):
    return pltpu.CompilerParams(vmem_limit_bytes=mib * 1024 * 1024)


def low_rows(value):
    return lax.broadcasted_iota(jnp.int32, value.shape, 1) < 4


def pack(tiles):
    t0, t1, t2, t3 = tiles
    e2, e3 = t2[:, :, TAIL:], t3[:, :, TAIL:]
    moved = jnp.concatenate([pltpu.roll(e2, 4, 1), e2, pltpu.roll(e3, 4, 1)], axis=2)
    last = t3[:, :, :TAIL]
    last = jnp.where(low_rows(last), last, moved)
    head = jnp.concatenate([t0, t1], axis=1)
    tail = jnp.concatenate([t2[:, :, :TAIL], last], axis=1)
    return head.astype(jnp.bfloat16), tail.astype(jnp.bfloat16)


def unpack(head, tail):
    head, tail = head.astype(jnp.float32), tail.astype(jnp.float32)
    t2, last = tail[:, :8], tail[:, 8:]
    m0, m1, m2 = last[:, :, :BLK], last[:, :, BLK : 2 * BLK], last[:, :, 2 * BLK :]
    e2 = jnp.where(low_rows(m0), pltpu.roll(m0, 4, 1), m1)
    e3 = pltpu.roll(m2, 4, 1)
    t2 = jnp.concatenate([t2, e2], axis=2)
    t3 = jnp.concatenate([last, e3], axis=2)
    t3 = jnp.where(low_rows(t3), t3, 0.0)
    return head[:, :8], head[:, 8:], t2, t3


def head_columns(n):
    return pl.ds(pl.multiple_of(n * CUT, CUT), CUT)


def tail_columns(n):
    return pl.ds(pl.multiple_of(FF + n * TAIL, BLK), TAIL)


def direction_kernel(grads_ref, momentum_ref, new_ref, out_ref):
    n = pl.program_id(0)
    grads = grads_ref[...].astype(jnp.float32)
    new = decay_rate * momentum_ref[...] + grads
    new_ref[...] = new
    direction = grads + decay_rate * new
    rows, mats, columns = direction.shape
    direction = jnp.concatenate([direction, jnp.zeros((PADROWS - rows, mats, columns), jnp.float32)], axis=0)
    head, tail = pack([jnp.swapaxes(direction[8 * t : 8 * t + 8], 0, 1) for t in range(4)])
    out_ref[:, :, head_columns(n)] = head
    out_ref[:, :, tail_columns(n)] = tail


def find_direction(grads, momentum):
    rows, mats = grads.shape[:2]
    cut = pl.BlockSpec((rows, mats, CUT), lambda n: (0, 0, n))
    return pl.pallas_call(
        direction_kernel,
        grid=(FF // CUT,),
        out_shape=(
            jax.ShapeDtypeStruct(grads.shape, jnp.float32),
            jax.ShapeDtypeStruct((mats, 16, PACKED), jnp.bfloat16),
        ),
        in_specs=[cut, cut],
        out_specs=(cut, pl.BlockSpec((mats, 16, PACKED), lambda n: (0, 0, 0))),
        compiler_params=room(60),
        name="find_direction",
    )(grads, momentum)


def spread_kernel(packed_ref, out_ref):
    n = pl.program_id(0)
    tiles = unpack(packed_ref[:, :, head_columns(n)], packed_ref[:, :, tail_columns(n)])
    rows = jnp.concatenate([jnp.swapaxes(t, 0, 1) for t in tiles], axis=0)
    out_ref[...] = rows[: out_ref.shape[0]].astype(jnp.bfloat16)


def spread_step(packed, rows):
    return pl.pallas_call(
        spread_kernel,
        grid=(FF // CUT,),
        out_shape=jax.ShapeDtypeStruct((rows, NZ, FF), jnp.bfloat16),
        in_specs=[pl.BlockSpec((NZ, 16, PACKED), lambda n: (0, 0, 0))],
        out_specs=pl.BlockSpec((rows, NZ, CUT), lambda n: (0, 0, n)),
        compiler_params=room(16),
        name="spread_step",
    )(packed)


def gram_kernel(place_ref, mine_ref, other_ref, *refs):
    shares, (x_ref, rows_ref) = refs[:8], refs[8:]
    core = place_ref[4]
    for n in range(FF // CUT):
        source = (n + 2 * core) % 4
        columns = pl.ds(n * CUT, CUT)
        for half, packed in enumerate((mine_ref, other_ref)):
            tiles = unpack(packed[:, :, head_columns(source)], packed[:, :, tail_columns(source)])
            rows = jnp.concatenate(tiles, axis=1).reshape(KROWS, CUT).astype(jnp.bfloat16)
            rows_ref[pl.ds(half * KROWS, KROWS), columns] = rows
            if half == 0:
                x_ref[:, columns] = rows
    for q in range(4):
        left = rows_ref[:, pl.ds(q * 2 * BLK, 2 * BLK)]
        right = rows_ref[:, pl.ds(q * 2 * BLK, BAND + BLK)]
        product = lax.dot_general(
            left, right, (((0,), (0,)), ((), ())), preferred_element_type=jnp.float32
        ).astype(jnp.bfloat16)
        first, second = product[:BLK, :BAND], product[BLK:, BLK:]

        @pl.when(place_ref[q] == 0)
        def _():
            shares[q][...] = first
            shares[4 + q][...] = second

        @pl.when(place_ref[q] == 1)
        def _():
            shares[q][...] = second
            shares[4 + q][...] = first


def gram_band(place, mine, other):
    return pl.pallas_call(
        gram_kernel,
        out_shape=[jax.ShapeDtypeStruct((BLK, BAND), jnp.bfloat16)] * 8
        + [jax.ShapeDtypeStruct((KROWS, FF), jnp.bfloat16)],
        in_specs=[SCALARS, MASS, MASS],
        out_specs=[MASS] * 9,
        scratch_shapes=[pltpu.VMEM((2 * KROWS, FF), jnp.bfloat16)],
        compiler_params=room(28),
        name="gram_band",
    )(place, mine, other)


def add(a, b):
    return (a.astype(jnp.float32) + b.astype(jnp.float32)).astype(jnp.bfloat16)


def halve_kernel(place_ref, *refs):
    mine, came, kept, sent = refs[:4], refs[4:8], refs[8:12], refs[12:]
    for q in range(4):
        bit = place_ref[q ^ 1]
        for out, at in ((kept[q], bit), (sent[q], 1 - bit)):
            rows = pl.ds(pl.multiple_of(at * HOLD, HOLD), HOLD)
            out[...] = add(mine[q][rows, :], came[q][rows, :])


def halve(place, mine, came):
    outs = pl.pallas_call(
        halve_kernel,
        out_shape=[jax.ShapeDtypeStruct((HOLD, BAND), jnp.bfloat16)] * 8,
        in_specs=[SCALARS] + [MASS] * 8,
        out_specs=[MASS] * 8,
        compiler_params=room(16),
        name="halve",
    )(place, *mine, *came)
    return outs[:4], outs[4:]


def add_kernel(*refs):
    for q in range(4):
        refs[8 + q][...] = add(refs[q][...], refs[4 + q][...])


def add_pairs(mine, came):
    return pl.pallas_call(
        add_kernel,
        out_shape=[jax.ShapeDtypeStruct((HOLD, BAND), jnp.bfloat16)] * 4,
        in_specs=[MASS] * 8,
        out_specs=[MASS] * 4,
        compiler_params=room(16),
        name="add_pairs",
    )(*mine, *came)


def join_kernel(place_ref, *refs):
    mine, came, outs = refs[:4], refs[4:8], refs[8:]
    for q in range(4):
        bit = place_ref[q ^ 1]
        for part, at in ((mine[q], bit), (came[q], 1 - bit)):
            outs[q][pl.ds(pl.multiple_of(at * HOLD, HOLD), HOLD), :] = part[...]


def join(place, mine, came):
    return pl.pallas_call(
        join_kernel,
        out_shape=[jax.ShapeDtypeStruct((BLK, BAND), jnp.bfloat16)] * 4,
        in_specs=[SCALARS] + [MASS] * 8,
        out_specs=[MASS] * 4,
        compiler_params=room(16),
        name="join",
    )(place, *mine, *came)


def step_kernel(place_ref, x_ref, *refs):
    pieces = refs[:16]
    out_ref, band_ref, gram_ref, first_ref, round_ref = refs[16:]
    core = place_ref[4]
    for side in range(2):
        for came in range(2):
            for q in range(4):
                bit = place_ref[q]
                at = 1 - bit if came else bit
                row = pl.multiple_of(side * HALF + (2 * q + at) * BLK, BLK)
                band_ref[pl.ds(row, BLK), :] = pieces[side * 8 + came * 4 + q][...]
    for i in range(NB):
        block = band_ref[pl.ds(i * BLK, BLK), :]
        turned = block[:, BLK : BAND - BLK].T
        for d in range(NB // 2 + 1):
            j = (i + d) % NB
            gram_ref[pl.ds(i * BLK, BLK), pl.ds(j * BLK, BLK)] = block[:, d * BLK : (d + 1) * BLK]
            if 1 <= d < NB // 2:
                gram_ref[pl.ds(j * BLK, BLK), pl.ds(i * BLK, BLK)] = turned[(d - 1) * BLK : d * BLK]

    def add_rows(k, total):
        part = jnp.abs(gram_ref[pl.ds(pl.multiple_of(k * 64, 64), 64), :].astype(jnp.float32))
        return total + jnp.sum(part.reshape(8, 8, FF), axis=0)

    sums = lax.fori_loop(0, FF // 64, add_rows, jnp.zeros((8, FF), jnp.float32))
    bound = jnp.max(jnp.sum(sums, axis=0, keepdims=True))
    bound = jnp.full((1, 1), bound, jnp.float32)
    inverse = 1.0 / bound
    scale = rms_match * math.sqrt(max(D, FF)) / jnp.sqrt(bound)
    for n in range(FF // CUT):
        columns = pl.ds(n * CUT, CUT)
        first = jnp.dot(x_ref[...], gram_ref[:, columns], preferred_element_type=jnp.float32) * inverse
        first_ref[:, columns] = linear_coef * x_ref[:, columns].astype(jnp.float32) + cubic_coef * first
        round_ref[:, columns] = first.astype(jnp.bfloat16)
    for n in range(FF // CUT):
        columns = pl.ds(n * CUT, CUT)
        second = jnp.dot(round_ref[...], gram_ref[:, columns], preferred_element_type=jnp.float32) * inverse
        step = scale * (first_ref[:, columns] + quintic_coef * second)
        step = step.reshape(NZ, PADROWS, CUT)
        head, tail = pack([step[:, 8 * t : 8 * t + 8] for t in range(4)])
        target = (n + 2 * core) % 4
        out_ref[:, :, head_columns(target)] = head
        out_ref[:, :, tail_columns(target)] = tail


def finish(place, mine, pieces):
    return pl.pallas_call(
        step_kernel,
        out_shape=jax.ShapeDtypeStruct((NZ, 16, PACKED), jnp.bfloat16),
        in_specs=[SCALARS] + [MASS] * 17,
        out_specs=MASS,
        scratch_shapes=[
            pltpu.VMEM((FF, BAND), jnp.bfloat16),
            pltpu.VMEM((FF, FF), jnp.bfloat16),
            pltpu.VMEM((KROWS, FF), jnp.float32),
            pltpu.VMEM((KROWS, FF), jnp.bfloat16),
        ],
        compiler_params=room(40),
        name="finish",
    )(place, mine, *pieces)


LINKS = (((0, 1), (1, 0), (2, 3), (3, 2)), ((0, 3), (3, 0), (1, 2), (2, 1)))


def trade(values, order):
    return [lax.ppermute(value, axis, LINKS[link]) for value, (axis, link) in zip(values, order)]


ALONG = (("x", 0), ("x", 1), ("y", 0), ("y", 1))
ALONG_NEXT = (("x", 1), ("x", 0), ("y", 1), ("y", 0))
ACROSS = (("y", 0), ("y", 1), ("x", 0), ("x", 1))
ACROSS_NEXT = (("y", 1), ("y", 0), ("x", 1), ("x", 0))


def swap_cores(value):
    return lax.ppermute(value, "c", [(0, 1), (1, 0)])


def largest(value, axes):
    for axis, size in axes:
        by = 1
        while by < size:
            other = lax.ppermute(value, axis, [(i, (i + by) % size) for i in range(size)])
            value = jnp.maximum(value, other)
            by *= 2
    return value


def body(grads, momentum, max_logits, q_weight, k_weight):
    x, y, core = lax.axis_index("x"), lax.axis_index("y"), lax.axis_index("c")
    place = jnp.stack([(x ^ (x >> 1)) & 1, x >> 1, (y ^ (y >> 1)) & 1, y >> 1, core]).astype(jnp.int32)
    rows = grads.shape[1]
    new_momentum, direction = find_direction(jnp.swapaxes(grads, 0, 1), jnp.swapaxes(momentum, 0, 1))
    new_momentum = jnp.swapaxes(new_momentum, 0, 1)
    direction, peak = lax.optimization_barrier((direction, max_logits))
    owned = lax.all_to_all(direction, "z", split_axis=0, concat_axis=0, tiled=True)
    peak = largest(peak, (("c", NC), ("x", NX), ("y", NY)))
    owned, peak = lax.optimization_barrier((owned, peak))
    *shares, mine = gram_band(place, owned, swap_cores(owned))
    kept, sent = halve(place, shares[:4], trade(shares[4:], ALONG))
    held = add_pairs(kept, trade(sent, ALONG_NEXT))
    held = add_pairs(held, trade(held, ACROSS))
    held = add_pairs(held, trade(held, ACROSS_NEXT))
    held = join(place, held, trade(held, ALONG_NEXT))
    held = list(held) + trade(held, ALONG)
    step = finish(place, mine, held + [swap_cores(piece) for piece in held])
    step, peak = lax.optimization_barrier((step, peak))
    step = lax.all_to_all(step, "z", split_axis=0, concat_axis=0, tiled=True)
    peak = largest(peak, (("z", NZ),))[0]
    step = jnp.swapaxes(spread_step(step, rows), 0, 1)

    gamma = jnp.minimum(1.0, clip_limit / peak)
    root = jnp.sqrt(gamma)
    local_heads = k_weight.shape[1] // NOPE
    first_head = lax.axis_index("z") * local_heads
    gamma_mine = lax.dynamic_slice_in_dim(gamma, first_head, local_heads)
    root_mine = lax.dynamic_slice_in_dim(root, first_head, local_heads)
    q_factor = jnp.concatenate(
        [
            jnp.broadcast_to(root_mine[:, None], (local_heads, NOPE)),
            jnp.broadcast_to(gamma_mine[:, None], (local_heads, ROPE)),
        ],
        axis=1,
    )
    q_view = q_weight.reshape(q_weight.shape[0], local_heads, NOPE + ROPE).astype(jnp.float32)
    q_clipped = (q_view * q_factor[None]).astype(jnp.bfloat16).reshape(q_weight.shape)
    k_view = k_weight.reshape(k_weight.shape[0], local_heads, NOPE).astype(jnp.float32)
    k_clipped = (k_view * root_mine[None, :, None]).astype(jnp.bfloat16).reshape(k_weight.shape)
    return (new_momentum, step, q_clipped, k_clipped)


def solution(mesh):
    split = Mesh(mesh.devices.reshape(NX, NY, NC, NZ), ("x", "y", "c", "z"))
    rows = P(None, ("x", "y", "c", "z"), None)
    heads = P(("x", "y", "c"), "z")
    return jax.shard_map(
        body,
        mesh=split,
        in_specs=(rows, rows, P(("x", "y", "c", "z"), None), heads, heads),
        out_specs=(rows, rows, heads, heads),
        check_vma=False,
    )
```

```python
import math

import jax
import jax.numpy as jnp
from jax import lax
from jax.experimental import pallas as pl
from jax.experimental.pallas import tpu as pltpu
from jax.sharding import Mesh, PartitionSpec as P

D = 7168
FF = 2048
NOPE = 128
ROPE = 64

decay_rate = 0.9
linear_coef = 3.4445
cubic_coef = -4.775
quintic_coef = 2.0315
clip_limit = 100.0
rms_match = 0.2

NX, NY, NC, NZ = 4, 4, 2, 8
PLANE = ("x", "y", "c")
BLK = 128
NB = FF // BLK
HALF = FF // 2
BAND = (NB // 2 + 1) * BLK
PADROWS = 32
KROWS = NZ * PADROWS
CUT = 512
TAIL = 384
PACKED = FF + (FF // CUT) * TAIL
QUARTER = 2 * BLK

MASS = pl.BlockSpec(memory_space=pltpu.VMEM)
SCALARS = pl.BlockSpec(memory_space=pltpu.SMEM)


def room(mib):
    return pltpu.CompilerParams(vmem_limit_bytes=mib * 1024 * 1024)


def low_rows(value):
    return lax.broadcasted_iota(jnp.int32, value.shape, 1) < 4


def pack(tiles):
    t0, t1, t2, t3 = tiles
    e2, e3 = t2[:, :, TAIL:], t3[:, :, TAIL:]
    moved = jnp.concatenate([pltpu.roll(e2, 4, 1), e2, pltpu.roll(e3, 4, 1)], axis=2)
    last = t3[:, :, :TAIL]
    last = jnp.where(low_rows(last), last, moved)
    head = jnp.concatenate([t0, t1], axis=1)
    tail = jnp.concatenate([t2[:, :, :TAIL], last], axis=1)
    return head.astype(jnp.bfloat16), tail.astype(jnp.bfloat16)


def unpack(head, tail):
    head, tail = head.astype(jnp.float32), tail.astype(jnp.float32)
    t2, last = tail[:, :8], tail[:, 8:]
    m0, m1, m2 = last[:, :, :BLK], last[:, :, BLK : 2 * BLK], last[:, :, 2 * BLK :]
    e2 = jnp.where(low_rows(m0), pltpu.roll(m0, 4, 1), m1)
    e3 = pltpu.roll(m2, 4, 1)
    t2 = jnp.concatenate([t2, e2], axis=2)
    t3 = jnp.concatenate([last, e3], axis=2)
    t3 = jnp.where(low_rows(t3), t3, 0.0)
    return head[:, :8], head[:, 8:], t2, t3


def head_columns(n):
    return pl.ds(pl.multiple_of(n * CUT, CUT), CUT)


def tail_columns(n):
    return pl.ds(pl.multiple_of(FF + n * TAIL, BLK), TAIL)


def direction_kernel(grads_ref, momentum_ref, out_ref):
    n = pl.program_id(0)
    grads = grads_ref[...].astype(jnp.float32)
    new = decay_rate * momentum_ref[...] + grads
    direction = grads + decay_rate * new
    rows, mats, columns = direction.shape
    direction = jnp.concatenate([direction, jnp.zeros((PADROWS - rows, mats, columns), jnp.float32)], axis=0)
    head, tail = pack([jnp.swapaxes(direction[8 * t : 8 * t + 8], 0, 1) for t in range(4)])
    out_ref[:, :, head_columns(n)] = head
    out_ref[:, :, tail_columns(n)] = tail


def find_direction(grads, momentum):
    rows, mats = grads.shape[:2]
    cut = pl.BlockSpec((rows, mats, CUT), lambda n: (0, 0, n))
    return pl.pallas_call(
        direction_kernel,
        grid=(FF // CUT,),
        out_shape=jax.ShapeDtypeStruct((mats, 16, PACKED), jnp.bfloat16),
        in_specs=[cut, cut],
        out_specs=pl.BlockSpec((mats, 16, PACKED), lambda n: (0, 0, 0)),
        compiler_params=room(60),
        name="find_direction",
    )(grads, momentum)


def spread_kernel(packed_ref, out_ref):
    n = pl.program_id(0)
    tiles = unpack(packed_ref[:, :, head_columns(n)], packed_ref[:, :, tail_columns(n)])
    rows = jnp.concatenate([jnp.swapaxes(t, 0, 1) for t in tiles], axis=0)
    out_ref[...] = rows[: out_ref.shape[0]].astype(jnp.bfloat16)


def spread_step(packed, rows):
    return pl.pallas_call(
        spread_kernel,
        grid=(FF // CUT,),
        out_shape=jax.ShapeDtypeStruct((rows, NZ, FF), jnp.bfloat16),
        in_specs=[pl.BlockSpec((NZ, 16, PACKED), lambda n: (0, 0, 0))],
        out_specs=pl.BlockSpec((rows, NZ, CUT), lambda n: (0, 0, n)),
        compiler_params=room(16),
        name="spread_step",
    )(packed)


def gram_kernel(place_ref, mine_ref, other_ref, *refs):
    shares, (x_ref, rows_ref, band_ref) = refs[:4], refs[4:]
    along, core = place_ref[0], place_ref[2]
    for n in range(FF // CUT):
        source = (n + 2 * core) % 4
        columns = pl.ds(n * CUT, CUT)
        for half, packed in enumerate((mine_ref, other_ref)):
            tiles = unpack(packed[:, :, head_columns(source)], packed[:, :, tail_columns(source)])
            rows = jnp.concatenate(tiles, axis=1).reshape(KROWS, CUT).astype(jnp.bfloat16)
            rows_ref[pl.ds(half * KROWS, KROWS), columns] = rows
            if half == 0:
                x_ref[:, columns] = rows
    for q in range(4):
        left = rows_ref[:, pl.ds(q * QUARTER, QUARTER)]
        right = rows_ref[:, pl.ds(q * QUARTER, BAND + BLK)]
        product = lax.dot_general(
            left, right, (((0,), (0,)), ((), ())), preferred_element_type=jnp.float32
        ).astype(jnp.bfloat16)
        for sub in range(2):
            band_ref[pl.ds(q * QUARTER + sub * BLK, BLK), :] = product[
                sub * BLK : (sub + 1) * BLK, sub * BLK : sub * BLK + BAND
            ]
    for d in range(4):
        shares[d][...] = band_ref[quarter_rows(along + d), :]


def quarter_rows(q, start=0):
    return pl.ds(pl.multiple_of(start + (q % 4) * QUARTER, QUARTER), QUARTER)


def gram_band(place, mine, other):
    return pl.pallas_call(
        gram_kernel,
        out_shape=[jax.ShapeDtypeStruct((QUARTER, BAND), jnp.bfloat16)] * 4
        + [jax.ShapeDtypeStruct((KROWS, FF), jnp.bfloat16)],
        in_specs=[SCALARS, MASS, MASS],
        out_specs=[MASS] * 5,
        scratch_shapes=[
            pltpu.VMEM((2 * KROWS, FF), jnp.bfloat16),
            pltpu.VMEM((HALF, BAND), jnp.bfloat16),
        ],
        compiler_params=room(28),
        name="gram_band",
    )(place, mine, other)


def quarter_kernel(*refs):
    parts, outs = refs[:4], refs[4:]
    for half in range(2):
        rows = pl.ds(half * BLK, BLK)
        total = sum(part[rows, :].astype(jnp.float32) for part in parts)
        outs[half][...] = total.astype(jnp.bfloat16)


def sum_quarter(parts):
    return pl.pallas_call(
        quarter_kernel,
        out_shape=[jax.ShapeDtypeStruct((BLK, BAND), jnp.bfloat16)] * 2,
        in_specs=[MASS] * 4,
        out_specs=[MASS] * 2,
        compiler_params=room(16),
        name="sum_quarter",
    )(*parts)


def pair_kernel(*refs):
    mine, came, outs = refs[:2], refs[2:4], refs[4:]
    for half in range(2):
        total = mine[half][...].astype(jnp.float32) + came[half][...].astype(jnp.float32)
        if len(outs) == 2:
            outs[half][...] = total.astype(jnp.bfloat16)
        else:
            outs[0][pl.ds(half * BLK, BLK), :] = total.astype(jnp.bfloat16)


def add_pairs(mine, came, joined):
    if joined:
        shapes = [jax.ShapeDtypeStruct((QUARTER, BAND), jnp.bfloat16)]
    else:
        shapes = [jax.ShapeDtypeStruct((BLK, BAND), jnp.bfloat16)] * 2
    return pl.pallas_call(
        pair_kernel,
        out_shape=shapes,
        in_specs=[MASS] * 4,
        out_specs=[MASS] * len(shapes),
        compiler_params=room(16),
        name="add_pairs",
    )(*mine, *came)


def step_kernel(place_ref, x_ref, *refs):
    pieces = refs[:8]
    out_ref, band_ref, gram_ref, first_ref, round_ref = refs[8:]
    core = place_ref[2]
    for side in range(2):
        for d in range(4):
            rows = quarter_rows(place_ref[side] + (4 - d), side * HALF)
            band_ref[rows, :] = pieces[side * 4 + d][...]
    for i in range(NB):
        block = band_ref[pl.ds(i * BLK, BLK), :]
        turned = block[:, BLK : BAND - BLK].T
        for d in range(NB // 2 + 1):
            j = (i + d) % NB
            gram_ref[pl.ds(i * BLK, BLK), pl.ds(j * BLK, BLK)] = block[:, d * BLK : (d + 1) * BLK]
            if 1 <= d < NB // 2:
                gram_ref[pl.ds(j * BLK, BLK), pl.ds(i * BLK, BLK)] = turned[(d - 1) * BLK : d * BLK]

    def add_rows(k, total):
        part = jnp.abs(gram_ref[pl.ds(pl.multiple_of(k * 64, 64), 64), :].astype(jnp.float32))
        return total + jnp.sum(part.reshape(8, 8, FF), axis=0)

    sums = lax.fori_loop(0, FF // 64, add_rows, jnp.zeros((8, FF), jnp.float32))
    bound = jnp.max(jnp.sum(sums, axis=0, keepdims=True))
    bound = jnp.full((1, 1), bound, jnp.float32)
    inverse = 1.0 / bound
    scale = rms_match * math.sqrt(max(D, FF)) / jnp.sqrt(bound)
    for n in range(FF // CUT):
        columns = pl.ds(n * CUT, CUT)
        first = jnp.dot(x_ref[...], gram_ref[:, columns], preferred_element_type=jnp.float32) * inverse
        first_ref[:, columns] = linear_coef * x_ref[:, columns].astype(jnp.float32) + cubic_coef * first
        round_ref[:, columns] = first.astype(jnp.bfloat16)
    for n in range(FF // CUT):
        columns = pl.ds(n * CUT, CUT)
        second = jnp.dot(round_ref[...], gram_ref[:, columns], preferred_element_type=jnp.float32) * inverse
        step = scale * (first_ref[:, columns] + quintic_coef * second)
        step = step.reshape(NZ, PADROWS, CUT)
        head, tail = pack([step[:, 8 * t : 8 * t + 8] for t in range(4)])
        target = (n + 2 * core) % 4
        out_ref[:, :, head_columns(target)] = head
        out_ref[:, :, tail_columns(target)] = tail


def finish(place, mine, pieces):
    return pl.pallas_call(
        step_kernel,
        out_shape=jax.ShapeDtypeStruct((NZ, 16, PACKED), jnp.bfloat16),
        in_specs=[SCALARS] + [MASS] * 9,
        out_specs=MASS,
        scratch_shapes=[
            pltpu.VMEM((FF, BAND), jnp.bfloat16),
            pltpu.VMEM((FF, FF), jnp.bfloat16),
            pltpu.VMEM((KROWS, FF), jnp.float32),
            pltpu.VMEM((KROWS, FF), jnp.bfloat16),
        ],
        compiler_params=room(40),
        name="finish",
    )(place, mine, *pieces)


def place_of(x, y, core):
    return (x * NY + y) * NC + core


def permutation(step):
    pairs = []
    for x in range(NX):
        for y in range(NY):
            for core in range(NC):
                mine = (x, y) if core == 0 else (y, x)
                to = step(*mine)
                to = to if core == 0 else to[::-1]
                pairs.append((place_of(x, y, core), place_of(*to, core)))
    return pairs


def send_along(value, by):
    return lax.ppermute(value, PLANE, permutation(lambda along, across: ((along + by) % 4, across)))


LINKS = ((1, 0, 3, 2), (3, 2, 1, 0))


def trade_across(values, first):
    links = (LINKS[first], LINKS[1 - first])
    return [
        lax.ppermute(value, PLANE, permutation(lambda along, across, link=link: (along, link[across])))
        for value, link in zip(values, links)
    ]


def collect(own, sends):
    came = {d: send_along(sends(d), d) for d in (2, 1, 3)}
    return [own, came[1], came[2], came[3]]


def swap_cores(value):
    return lax.ppermute(value, "c", [(0, 1), (1, 0)])


def largest(value, axis, by, size):
    return jnp.maximum(value, lax.ppermute(value, axis, [(i, (i + by) % size) for i in range(size)]))


def body(grads, momentum, max_logits, q_weight, k_weight):
    x, y, core = lax.axis_index("x"), lax.axis_index("y"), lax.axis_index("c")
    place = jnp.stack([jnp.where(core == 0, x, y), jnp.where(core == 0, y, x), core]).astype(jnp.int32)
    rows = grads.shape[1]
    direction = find_direction(jnp.swapaxes(grads, 0, 1), jnp.swapaxes(momentum, 0, 1))
    direction, peak, grads, momentum = lax.optimization_barrier((direction, max_logits, grads, momentum))
    owned = lax.all_to_all(direction, "z", split_axis=0, concat_axis=0, tiled=True)
    new_momentum = decay_rate * momentum + grads.astype(jnp.float32)
    for axis, by, size in (("c", 1, NC), ("x", 1, NX), ("x", 2, NX), ("y", 1, NY), ("y", 2, NY)):
        peak = largest(peak, axis, by, size)
    owned, peak, new_momentum = lax.optimization_barrier((owned, peak, new_momentum))
    *shares, mine = gram_band(place, owned, swap_cores(owned))
    shares[0], peak = lax.optimization_barrier((shares[0], peak))
    parts = collect(shares[0], lambda d: shares[d])
    for by in (1, 2):
        peak = largest(peak, "z", by, NZ)
    parts[0], peak = lax.optimization_barrier((parts[0], peak))
    held = sum_quarter(parts)
    held = add_pairs(held, trade_across(held, 0), False)
    held, = add_pairs(held, trade_across(held, 1), True)
    held, peak = lax.optimization_barrier((held, peak))
    pieces = collect(held, lambda d: held)
    peak = largest(peak, "z", 4, NZ)
    pieces[0], pieces[2], peak = lax.optimization_barrier((pieces[0], pieces[2], peak))
    other = [swap_cores(piece) for piece in pieces]
    step = finish(place, mine, pieces + other)
    step, peak, q_weight, k_weight = lax.optimization_barrier((step, peak, q_weight, k_weight))
    step = lax.all_to_all(step, "z", split_axis=0, concat_axis=0, tiled=True)
    peak = peak[0]

    gamma = jnp.minimum(1.0, clip_limit / peak)
    root = jnp.sqrt(gamma)
    local_heads = k_weight.shape[1] // NOPE
    first_head = lax.axis_index("z") * local_heads
    gamma_mine = lax.dynamic_slice_in_dim(gamma, first_head, local_heads)
    root_mine = lax.dynamic_slice_in_dim(root, first_head, local_heads)
    q_factor = jnp.concatenate(
        [
            jnp.broadcast_to(root_mine[:, None], (local_heads, NOPE)),
            jnp.broadcast_to(gamma_mine[:, None], (local_heads, ROPE)),
        ],
        axis=1,
    )
    q_view = q_weight.reshape(q_weight.shape[0], local_heads, NOPE + ROPE).astype(jnp.float32)
    q_clipped = (q_view * q_factor[None]).astype(jnp.bfloat16).reshape(q_weight.shape)
    k_view = k_weight.reshape(k_weight.shape[0], local_heads, NOPE).astype(jnp.float32)
    k_clipped = (k_view * root_mine[None, :, None]).astype(jnp.bfloat16).reshape(k_weight.shape)
    step, q_clipped, k_clipped = lax.optimization_barrier((step, q_clipped, k_clipped))
    step = jnp.swapaxes(spread_step(step, rows), 0, 1)
    return (new_momentum, step, q_clipped, k_clipped)


def solution(mesh):
    split = Mesh(mesh.devices.reshape(NX, NY, NC, NZ), ("x", "y", "c", "z"))
    rows = P(None, ("x", "y", "c", "z"), None)
    heads = P(("x", "y", "c"), "z")
    return jax.shard_map(
        body,
        mesh=split,
        in_specs=(rows, rows, P(("x", "y", "c", "z"), None), heads, heads),
        out_specs=(rows, rows, heads, heads),
        check_vma=False,
    )
```

```python
import math

import jax
import jax.numpy as jnp
from jax import lax
from jax.experimental import pallas as pl
from jax.experimental.pallas import tpu as pltpu
from jax.sharding import Mesh, PartitionSpec as P

D = 7168
FF = 2048
NOPE = 128
ROPE = 64

decay_rate = 0.9
linear_coef = 3.4445
cubic_coef = -4.775
quintic_coef = 2.0315
clip_limit = 100.0
rms_match = 0.2

NX, NY, NC, NZ = 4, 4, 2, 8
PLANE = ("x", "y", "c")
BLK = 128
NB = FF // BLK
HALF = FF // 2
BAND = (NB // 2 + 1) * BLK
PADROWS = 32
KROWS = NZ * PADROWS
CUT = 512
TAIL = 384
PACKED = FF + (FF // CUT) * TAIL
QUARTER = 2 * BLK

MASS = pl.BlockSpec(memory_space=pltpu.VMEM)
SCALARS = pl.BlockSpec(memory_space=pltpu.SMEM)


def room(mib):
    return pltpu.CompilerParams(vmem_limit_bytes=mib * 1024 * 1024)


def low_rows(value):
    return lax.broadcasted_iota(jnp.int32, value.shape, 1) < 4


def pack(tiles):
    t0, t1, t2, t3 = tiles
    e2, e3 = t2[:, :, TAIL:], t3[:, :, TAIL:]
    moved = jnp.concatenate([pltpu.roll(e2, 4, 1), e2, pltpu.roll(e3, 4, 1)], axis=2)
    last = t3[:, :, :TAIL]
    last = jnp.where(low_rows(last), last, moved)
    head = jnp.concatenate([t0, t1], axis=1)
    tail = jnp.concatenate([t2[:, :, :TAIL], last], axis=1)
    return head.astype(jnp.bfloat16), tail.astype(jnp.bfloat16)


def unpack(head, tail):
    head, tail = head.astype(jnp.float32), tail.astype(jnp.float32)
    t2, last = tail[:, :8], tail[:, 8:]
    m0, m1, m2 = last[:, :, :BLK], last[:, :, BLK : 2 * BLK], last[:, :, 2 * BLK :]
    e2 = jnp.where(low_rows(m0), pltpu.roll(m0, 4, 1), m1)
    e3 = pltpu.roll(m2, 4, 1)
    t2 = jnp.concatenate([t2, e2], axis=2)
    t3 = jnp.concatenate([last, e3], axis=2)
    t3 = jnp.where(low_rows(t3), t3, 0.0)
    return head[:, :8], head[:, 8:], t2, t3


def head_columns(n):
    return pl.ds(pl.multiple_of(n * CUT, CUT), CUT)


def tail_columns(n):
    return pl.ds(pl.multiple_of(FF + n * TAIL, BLK), TAIL)


def direction_kernel(place_ref, grads_ref, momentum_ref, *refs):
    outs, (grads_buf, momentum_buf, packed_ref, grads_sem, momentum_sem) = refs[:NZ], refs[NZ:]
    z = place_ref[3]
    copies = []
    for n in range(FF // CUT):
        columns = pl.ds(n * CUT, CUT)
        pair = (
            pltpu.make_async_copy(momentum_ref.at[:, :, columns], momentum_buf.at[n], momentum_sem.at[n]),
            pltpu.make_async_copy(grads_ref.at[:, :, columns], grads_buf.at[n], grads_sem.at[n]),
        )
        for copy in pair:
            copy.start()
        copies.append(pair)
    for n in range(FF // CUT):
        for copy in copies[n]:
            copy.wait()
        grads = grads_buf[n].astype(jnp.float32)
        direction = grads + decay_rate * (decay_rate * momentum_buf[n] + grads)
        rows, mats, columns = direction.shape
        direction = jnp.concatenate([direction, jnp.zeros((PADROWS - rows, mats, columns), jnp.float32)], axis=0)
        head, tail = pack([jnp.swapaxes(direction[8 * t : 8 * t + 8], 0, 1) for t in range(4)])
        packed_ref[:, :, head_columns(n)] = head
        packed_ref[:, :, tail_columns(n)] = tail
    for d in range(NZ):
        outs[d][...] = packed_ref[(z + d) % NZ]


BLOCKS = [jax.ShapeDtypeStruct((16, PACKED), jnp.bfloat16)] * NZ


def find_direction(place, grads, momentum):
    rows, mats = grads.shape[:2]
    cuts = FF // CUT
    return pl.pallas_call(
        direction_kernel,
        out_shape=BLOCKS,
        in_specs=[SCALARS] + [pl.BlockSpec(memory_space=pl.ANY)] * 2,
        out_specs=[MASS] * NZ,
        scratch_shapes=[
            pltpu.VMEM((cuts, rows, mats, CUT), jnp.bfloat16),
            pltpu.VMEM((cuts, rows, mats, CUT), jnp.float32),
            pltpu.VMEM((mats, 16, PACKED), jnp.bfloat16),
            pltpu.SemaphoreType.DMA((cuts,)),
            pltpu.SemaphoreType.DMA((cuts,)),
        ],
        compiler_params=room(60),
        name="find_direction",
    )(place, grads, momentum)


def spread_kernel(place_ref, *refs):
    blocks, (out_ref, packed_ref, rows_ref, sem) = refs[:NZ], refs[NZ:]
    z = place_ref[3]
    for d in range(NZ):
        packed_ref[(z + d) % NZ] = blocks[d][...]
    copies = []
    for n in range(FF // CUT):
        tiles = unpack(packed_ref[:, :, head_columns(n)], packed_ref[:, :, tail_columns(n)])
        rows = jnp.concatenate([jnp.swapaxes(t, 0, 1) for t in tiles], axis=0)
        rows_ref[n] = rows[: out_ref.shape[0]].astype(jnp.bfloat16)
        copy = pltpu.make_async_copy(rows_ref.at[n], out_ref.at[:, :, pl.ds(n * CUT, CUT)], sem.at[n])
        copy.start()
        copies.append(copy)
    for copy in copies:
        copy.wait()


def spread_step(place, blocks, rows):
    cuts = FF // CUT
    return pl.pallas_call(
        spread_kernel,
        out_shape=jax.ShapeDtypeStruct((rows, NZ, FF), jnp.bfloat16),
        in_specs=[SCALARS] + [MASS] * NZ,
        out_specs=pl.BlockSpec(memory_space=pl.ANY),
        scratch_shapes=[
            pltpu.VMEM((NZ, 16, PACKED), jnp.bfloat16),
            pltpu.VMEM((cuts, rows, NZ, CUT), jnp.bfloat16),
            pltpu.SemaphoreType.DMA((cuts,)),
        ],
        compiler_params=room(16),
        name="spread_step",
    )(place, *blocks)


def gram_kernel(place_ref, *refs):
    blocks, shares, (x_ref, rows_ref, band_ref) = refs[: 2 * NZ], refs[2 * NZ : 2 * NZ + 4], refs[2 * NZ + 4 :]
    along, core = place_ref[0], place_ref[2]
    for n in range(FF // CUT):
        source = (n + 2 * core) % 4
        columns = pl.ds(n * CUT, CUT)
        for half in range(2):
            packed = blocks[half * NZ : (half + 1) * NZ]
            head = jnp.stack([block[:, head_columns(source)] for block in packed])
            tail = jnp.stack([block[:, tail_columns(source)] for block in packed])
            tiles = unpack(head, tail)
            rows = jnp.concatenate(tiles, axis=1).reshape(KROWS, CUT).astype(jnp.bfloat16)
            rows_ref[pl.ds(half * KROWS, KROWS), columns] = rows
            if half == 0:
                x_ref[:, columns] = rows
    for q in range(4):
        left = rows_ref[:, pl.ds(q * QUARTER, QUARTER)]
        right = rows_ref[:, pl.ds(q * QUARTER, BAND + BLK)]
        product = lax.dot_general(
            left, right, (((0,), (0,)), ((), ())), preferred_element_type=jnp.float32
        ).astype(jnp.bfloat16)
        for sub in range(2):
            band_ref[pl.ds(q * QUARTER + sub * BLK, BLK), :] = product[
                sub * BLK : (sub + 1) * BLK, sub * BLK : sub * BLK + BAND
            ]
    for d in range(4):
        shares[d][...] = band_ref[quarter_rows(along + d), :]


def quarter_rows(q, start=0):
    return pl.ds(pl.multiple_of(start + (q % 4) * QUARTER, QUARTER), QUARTER)


def gram_band(place, blocks):
    return pl.pallas_call(
        gram_kernel,
        out_shape=[jax.ShapeDtypeStruct((QUARTER, BAND), jnp.bfloat16)] * 4
        + [jax.ShapeDtypeStruct((KROWS, FF), jnp.bfloat16)],
        in_specs=[SCALARS] + [MASS] * (2 * NZ),
        out_specs=[MASS] * 5,
        scratch_shapes=[
            pltpu.VMEM((2 * KROWS, FF), jnp.bfloat16),
            pltpu.VMEM((HALF, BAND), jnp.bfloat16),
        ],
        compiler_params=room(28),
        name="gram_band",
    )(place, *blocks)


def quarter_kernel(*refs):
    parts, outs = refs[:4], refs[4:]
    for half in range(2):
        rows = pl.ds(half * BLK, BLK)
        total = sum(part[rows, :].astype(jnp.float32) for part in parts)
        outs[half][...] = total.astype(jnp.bfloat16)


def sum_quarter(parts):
    return pl.pallas_call(
        quarter_kernel,
        out_shape=[jax.ShapeDtypeStruct((BLK, BAND), jnp.bfloat16)] * 2,
        in_specs=[MASS] * 4,
        out_specs=[MASS] * 2,
        compiler_params=room(16),
        name="sum_quarter",
    )(*parts)


def pair_kernel(*refs):
    mine, came, outs = refs[:2], refs[2:4], refs[4:]
    for half in range(2):
        total = mine[half][...].astype(jnp.float32) + came[half][...].astype(jnp.float32)
        if len(outs) == 2:
            outs[half][...] = total.astype(jnp.bfloat16)
        else:
            outs[0][pl.ds(half * BLK, BLK), :] = total.astype(jnp.bfloat16)


def add_pairs(mine, came, joined):
    if joined:
        shapes = [jax.ShapeDtypeStruct((QUARTER, BAND), jnp.bfloat16)]
    else:
        shapes = [jax.ShapeDtypeStruct((BLK, BAND), jnp.bfloat16)] * 2
    return pl.pallas_call(
        pair_kernel,
        out_shape=shapes,
        in_specs=[MASS] * 4,
        out_specs=[MASS] * len(shapes),
        compiler_params=room(16),
        name="add_pairs",
    )(*mine, *came)


def step_kernel(place_ref, x_ref, *refs):
    pieces = refs[:8]
    outs, (band_ref, gram_ref, first_ref, round_ref) = refs[8 : 8 + NZ], refs[8 + NZ :]
    core = place_ref[2]
    for side in range(2):
        for d in range(4):
            rows = quarter_rows(place_ref[side] + (4 - d), side * HALF)
            band_ref[rows, :] = pieces[side * 4 + d][...]
    for i in range(NB):
        block = band_ref[pl.ds(i * BLK, BLK), :]
        turned = block[:, BLK : BAND - BLK].T
        for d in range(NB // 2 + 1):
            j = (i + d) % NB
            gram_ref[pl.ds(i * BLK, BLK), pl.ds(j * BLK, BLK)] = block[:, d * BLK : (d + 1) * BLK]
            if 1 <= d < NB // 2:
                gram_ref[pl.ds(j * BLK, BLK), pl.ds(i * BLK, BLK)] = turned[(d - 1) * BLK : d * BLK]

    ones = jnp.ones((16, FF), jnp.bfloat16)
    bound = jnp.zeros((1, 1), jnp.float32)
    for n in range(FF // CUT):
        columns = pl.ds(n * CUT, CUT)
        gram = gram_ref[:, columns]
        first_ref[:, columns] = jnp.dot(x_ref[...], gram, preferred_element_type=jnp.float32)
        sums = jnp.dot(ones, jnp.abs(gram), preferred_element_type=jnp.float32)
        bound = jnp.maximum(bound, jnp.max(sums[:8], keepdims=True))
    inverse = 1.0 / bound
    scale = rms_match * math.sqrt(max(D, FF)) / jnp.sqrt(bound)
    for n in range(FF // CUT):
        columns = pl.ds(n * CUT, CUT)
        first = first_ref[:, columns] * inverse
        round_ref[:, columns] = first.astype(jnp.bfloat16)
        first_ref[:, columns] = linear_coef * x_ref[:, columns].astype(jnp.float32) + cubic_coef * first
    for n in range(FF // CUT):
        columns = pl.ds(n * CUT, CUT)
        second = jnp.dot(round_ref[...], gram_ref[:, columns], preferred_element_type=jnp.float32) * inverse
        step = scale * (first_ref[:, columns] + quintic_coef * second)
        step = step.reshape(NZ, PADROWS, CUT)
        head, tail = pack([step[:, 8 * t : 8 * t + 8] for t in range(4)])
        target = (n + 2 * core) % 4
        for d in range(NZ):
            outs[d][:, head_columns(target)] = head[d]
            outs[d][:, tail_columns(target)] = tail[d]


def finish(place, mine, pieces):
    return pl.pallas_call(
        step_kernel,
        out_shape=BLOCKS,
        in_specs=[SCALARS] + [MASS] * 9,
        out_specs=[MASS] * NZ,
        scratch_shapes=[
            pltpu.VMEM((FF, BAND), jnp.bfloat16),
            pltpu.VMEM((FF, FF), jnp.bfloat16),
            pltpu.VMEM((KROWS, FF), jnp.float32),
            pltpu.VMEM((KROWS, FF), jnp.bfloat16),
        ],
        compiler_params=room(40),
        name="finish",
    )(place, mine, *pieces)


def place_of(x, y, core):
    return (x * NY + y) * NC + core


def permutation(step):
    pairs = []
    for x in range(NX):
        for y in range(NY):
            for core in range(NC):
                mine = (x, y) if core == 0 else (y, x)
                to = step(*mine)
                to = to if core == 0 else to[::-1]
                pairs.append((place_of(x, y, core), place_of(*to, core)))
    return pairs


def send_along(value, by):
    return lax.ppermute(value, PLANE, permutation(lambda along, across: ((along + by) % 4, across)))


LINKS = ((1, 0, 3, 2), (3, 2, 1, 0))


def trade_across(values, first):
    links = (LINKS[first], LINKS[1 - first])
    return [
        lax.ppermute(value, PLANE, permutation(lambda along, across, link=link: (along, link[across])))
        for value, link in zip(values, links)
    ]


def collect(own, sends):
    came = {d: send_along(sends(d), d) for d in (2, 1, 3)}
    return [own, came[1], came[2], came[3]]


def swap_cores(value):
    return lax.ppermute(value, "c", [(0, 1), (1, 0)])


def trade_planes(blocks, sign):
    came = [blocks[0]] + [None] * (NZ - 1)
    for d in (4, 3, 5, 2, 6, 1, 7):
        came[d] = lax.ppermute(blocks[d], "z", [(i, (i + sign * d) % NZ) for i in range(NZ)])
    return came


def turned(value, axis, by, size):
    return lax.ppermute(value, axis, [(i, (i + by) % size) for i in range(size)])


def largest(value, axis):
    others = [turned(value, axis, by, 4) for by in (2, 1, 3)]
    return jnp.maximum(jnp.maximum(value, others[0]), jnp.maximum(others[1], others[2]))


def body(grads, momentum, max_logits, q_weight, k_weight):
    x, y, core = lax.axis_index("x"), lax.axis_index("y"), lax.axis_index("c")
    along, across = jnp.where(core == 0, x, y), jnp.where(core == 0, y, x)
    place = jnp.stack([along, across, core, lax.axis_index("z")]).astype(jnp.int32)
    rows = grads.shape[1]
    blocks = list(find_direction(place, jnp.swapaxes(grads, 0, 1), jnp.swapaxes(momentum, 0, 1)))
    blocks[0], grads, momentum = lax.optimization_barrier((blocks[0], grads, momentum))
    owned = trade_planes(blocks, 1)
    owned[4], peak = lax.optimization_barrier((owned[4], max_logits))
    peak = largest(peak, "y")
    new_momentum = decay_rate * momentum + grads.astype(jnp.float32)
    other = [None] * NZ
    for d in (0, 4, 3, 5, 2, 6, 1, 7):
        other[d] = swap_cores(owned[d])
    owned[0], peak, new_momentum = lax.optimization_barrier((owned[0], peak, new_momentum))
    *shares, mine = gram_band(place, owned + other)
    shares[0], peak = lax.optimization_barrier((shares[0], peak))
    parts = collect(shares[0], lambda d: shares[d])
    for by in (1, 2):
        peak = jnp.maximum(peak, turned(peak, "z", by, NZ))
    parts[0], peak = lax.optimization_barrier((parts[0], peak))
    held = sum_quarter(parts)
    came = trade_across(held, 0)
    came[0], peak = lax.optimization_barrier((came[0], jnp.maximum(peak, swap_cores(peak))))
    held = add_pairs(held, came, False)
    held, = add_pairs(held, trade_across(held, 1), True)
    held, peak = lax.optimization_barrier((held, peak))
    pieces = collect(held, lambda d: held)
    peak = jnp.maximum(peak, turned(peak, "z", 4, NZ))
    pieces[0], pieces[2], peak = lax.optimization_barrier((pieces[0], pieces[2], peak))
    other = [swap_cores(piece) for piece in pieces]
    step = list(finish(place, mine, pieces + other))
    step[0], peak, q_weight, k_weight = lax.optimization_barrier((step[0], peak, q_weight, k_weight))
    step = trade_planes(step, -1)
    step[4], peak = lax.optimization_barrier((step[4], peak))
    peak = largest(peak, "x")
    peak = peak[0]

    gamma = jnp.minimum(1.0, clip_limit / peak)
    root = jnp.sqrt(gamma)
    local_heads = k_weight.shape[1] // NOPE
    first_head = lax.axis_index("z") * local_heads
    gamma_mine = lax.dynamic_slice_in_dim(gamma, first_head, local_heads)
    root_mine = lax.dynamic_slice_in_dim(root, first_head, local_heads)
    q_factor = jnp.concatenate(
        [
            jnp.broadcast_to(root_mine[:, None], (local_heads, NOPE)),
            jnp.broadcast_to(gamma_mine[:, None], (local_heads, ROPE)),
        ],
        axis=1,
    )
    q_view = q_weight.reshape(q_weight.shape[0], local_heads, NOPE + ROPE).astype(jnp.float32)
    q_clipped = (q_view * q_factor[None]).astype(jnp.bfloat16).reshape(q_weight.shape)
    k_view = k_weight.reshape(k_weight.shape[0], local_heads, NOPE).astype(jnp.float32)
    k_clipped = (k_view * root_mine[None, :, None]).astype(jnp.bfloat16).reshape(k_weight.shape)
    step[0], q_clipped, k_clipped = lax.optimization_barrier((step[0], q_clipped, k_clipped))
    step = jnp.swapaxes(spread_step(place, step, rows), 0, 1)
    return (new_momentum, step, q_clipped, k_clipped)


def solution(mesh):
    split = Mesh(mesh.devices.reshape(NX, NY, NC, NZ), ("x", "y", "c", "z"))
    rows = P(None, ("x", "y", "c", "z"), None)
    heads = P(("x", "y", "c"), "z")
    return jax.shard_map(
        body,
        mesh=split,
        in_specs=(rows, rows, P(("x", "y", "c", "z"), None), heads, heads),
        out_specs=(rows, rows, heads, heads),
        check_vma=False,
    )
```

```python
import math

import jax
import jax.numpy as jnp
from jax import lax
from jax.experimental import pallas as pl
from jax.experimental.pallas import tpu as pltpu
from jax.sharding import Mesh, PartitionSpec as P

D = 7168
FF = 2048
NOPE = 128
ROPE = 64

decay_rate = 0.9
linear_coef = 3.4445
cubic_coef = -4.775
quintic_coef = 2.0315
clip_limit = 100.0
rms_match = 0.2

NX, NY, NC, NZ = 4, 4, 2, 8
PLANE = ("x", "y", "c")
BLK = 128
NB = FF // BLK
HALF = FF // 2
BAND = (NB // 2 + 1) * BLK
PADROWS = 32
KROWS = NZ * PADROWS
CUT = 512
TAIL = 384
PACKED = FF + (FF // CUT) * TAIL
WIDTH = PACKED + BLK
EXTRA = 16
QUARTER = 2 * BLK

MASS = pl.BlockSpec(memory_space=pltpu.VMEM)
SCALARS = pl.BlockSpec(memory_space=pltpu.SMEM)
FAR = pl.BlockSpec(memory_space=pl.ANY)


def room(mib):
    return pltpu.CompilerParams(vmem_limit_bytes=mib * 1024 * 1024)


def low_rows(value):
    return lax.broadcasted_iota(jnp.int32, value.shape, 1) < 4


def pack(tiles):
    t0, t1, t2, t3 = tiles
    e2, e3 = t2[:, :, TAIL:], t3[:, :, TAIL:]
    moved = jnp.concatenate([pltpu.roll(e2, 4, 1), e2, pltpu.roll(e3, 4, 1)], axis=2)
    last = t3[:, :, :TAIL]
    last = jnp.where(low_rows(last), last, moved)
    head = jnp.concatenate([t0, t1], axis=1)
    tail = jnp.concatenate([t2[:, :, :TAIL], last], axis=1)
    return head.astype(jnp.bfloat16), tail.astype(jnp.bfloat16)


def unpack(head, tail):
    head, tail = head.astype(jnp.float32), tail.astype(jnp.float32)
    t2, last = tail[:, :8], tail[:, 8:]
    m0, m1, m2 = last[:, :, :BLK], last[:, :, BLK : 2 * BLK], last[:, :, 2 * BLK :]
    e2 = jnp.where(low_rows(m0), pltpu.roll(m0, 4, 1), m1)
    e3 = pltpu.roll(m2, 4, 1)
    t2 = jnp.concatenate([t2, e2], axis=2)
    t3 = jnp.concatenate([last, e3], axis=2)
    t3 = jnp.where(low_rows(t3), t3, 0.0)
    return head[:, :8], head[:, 8:], t2, t3


def split_terms(value):
    high = value.astype(jnp.bfloat16).astype(jnp.float32)
    rest = value - high
    middle = rest.astype(jnp.bfloat16).astype(jnp.float32)
    row = lax.broadcasted_iota(jnp.int32, (EXTRA, BLK), 0)
    tile = jnp.where(row == 0, high, jnp.where(row == 1, middle, jnp.where(row == 2, rest - middle, 0.0)))
    return tile.astype(jnp.bfloat16)


def largest(tiles):
    best = None
    for tile in tiles:
        tile = tile.astype(jnp.float32)
        value = tile[0:1] + tile[1:2] + tile[2:3]
        best = value if best is None else jnp.maximum(best, value)
    return best


def head_columns(n):
    return pl.ds(pl.multiple_of(n * CUT, CUT), CUT)


def tail_columns(n):
    return pl.ds(pl.multiple_of(FF + n * TAIL, BLK), TAIL)


def direction_kernel(logits_ref, grads_ref, momentum_ref, *refs):
    outs, (grads_buf, momentum_buf, packed_ref, grads_sem, momentum_sem) = refs[:NZ], refs[NZ:]
    z = lax.axis_index("z")
    copies = []
    for n in range(FF // CUT):
        columns = pl.ds(n * CUT, CUT)
        pair = (
            pltpu.make_async_copy(momentum_ref.at[:, :, columns], momentum_buf.at[n], momentum_sem.at[n]),
            pltpu.make_async_copy(grads_ref.at[:, :, columns], grads_buf.at[n], grads_sem.at[n]),
        )
        for copy in pair:
            copy.start()
        copies.append(pair)
    for n in range(FF // CUT):
        for copy in copies[n]:
            copy.wait()
        grads = grads_buf[n].astype(jnp.float32)
        direction = grads + decay_rate * (decay_rate * momentum_buf[n] + grads)
        rows, mats, columns = direction.shape
        direction = jnp.concatenate([direction, jnp.zeros((PADROWS - rows, mats, columns), jnp.float32)], axis=0)
        head, tail = pack([jnp.swapaxes(direction[8 * t : 8 * t + 8], 0, 1) for t in range(4)])
        packed_ref[:, :, head_columns(n)] = head
        packed_ref[:, :, tail_columns(n)] = tail
    logits = logits_ref[...]
    terms = split_terms(jnp.concatenate([logits, jnp.zeros((1, BLK - logits.shape[1]), jnp.float32)], axis=1))
    for d in range(NZ):
        outs[d][:, :PACKED] = packed_ref[(z + d) % NZ]
        outs[d][:, PACKED:] = terms


def find_direction(logits, grads, momentum):
    rows, mats = grads.shape[:2]
    cuts = FF // CUT
    return pl.pallas_call(
        direction_kernel,
        out_shape=[jax.ShapeDtypeStruct((16, WIDTH), jnp.bfloat16)] * NZ,
        in_specs=[MASS] + [FAR] * 2,
        out_specs=[MASS] * NZ,
        scratch_shapes=[
            pltpu.VMEM((cuts, rows, mats, CUT), jnp.bfloat16),
            pltpu.VMEM((cuts, rows, mats, CUT), jnp.float32),
            pltpu.VMEM((mats, 16, PACKED), jnp.bfloat16),
            pltpu.SemaphoreType.DMA((cuts,)),
            pltpu.SemaphoreType.DMA((cuts,)),
        ],
        compiler_params=room(60),
        name="find_direction",
    )(logits, grads, momentum)


def momentum_kernel(grads_ref, momentum_ref, out_ref, grads_buf, momentum_buf, in_sem, out_sem):
    copies = []
    for n in range(FF // CUT):
        columns = pl.ds(n * CUT, CUT)
        trio = (
            pltpu.make_async_copy(momentum_ref.at[:, :, columns], momentum_buf.at[n], in_sem.at[0, n]),
            pltpu.make_async_copy(grads_ref.at[:, :, columns], grads_buf.at[n], in_sem.at[1, n]),
            pltpu.make_async_copy(momentum_buf.at[n], out_ref.at[:, :, columns], out_sem.at[n]),
        )
        trio[0].start()
        trio[1].start()
        copies.append(trio)
    for n in range(FF // CUT):
        copies[n][0].wait()
        copies[n][1].wait()
        momentum_buf[n] = decay_rate * momentum_buf[n] + grads_buf[n].astype(jnp.float32)
        copies[n][2].start()
    for trio in copies:
        trio[2].wait()


def add_momentum(grads, momentum):
    rows, mats = grads.shape[:2]
    cuts = FF // CUT
    return pl.pallas_call(
        momentum_kernel,
        out_shape=jax.ShapeDtypeStruct(grads.shape, jnp.float32),
        in_specs=[FAR] * 2,
        out_specs=FAR,
        scratch_shapes=[
            pltpu.VMEM((cuts, rows, mats, CUT), jnp.bfloat16),
            pltpu.VMEM((cuts, rows, mats, CUT), jnp.float32),
            pltpu.SemaphoreType.DMA((2, cuts)),
            pltpu.SemaphoreType.DMA((cuts,)),
        ],
        compiler_params=room(58),
        name="add_momentum",
    )(grads, momentum)


def spread_kernel(place_ref, *refs):
    blocks, (out_ref, packed_ref, rows_ref, sem) = refs[:NZ], refs[NZ:]
    z = place_ref[3]
    for d in range(NZ):
        packed_ref[(z + d) % NZ] = blocks[d][...]
    copies = []
    for n in range(FF // CUT):
        tiles = unpack(packed_ref[:, :, head_columns(n)], packed_ref[:, :, tail_columns(n)])
        rows = jnp.concatenate([jnp.swapaxes(t, 0, 1) for t in tiles], axis=0)
        rows_ref[n] = rows[: out_ref.shape[0]].astype(jnp.bfloat16)
        copy = pltpu.make_async_copy(rows_ref.at[n], out_ref.at[:, :, pl.ds(n * CUT, CUT)], sem.at[n])
        copy.start()
        copies.append(copy)
    for copy in copies:
        copy.wait()


def spread_step(place, blocks, rows):
    cuts = FF // CUT
    return pl.pallas_call(
        spread_kernel,
        out_shape=jax.ShapeDtypeStruct((rows, NZ, FF), jnp.bfloat16),
        in_specs=[SCALARS] + [MASS] * NZ,
        out_specs=pl.BlockSpec(memory_space=pl.ANY),
        scratch_shapes=[
            pltpu.VMEM((NZ, 16, PACKED), jnp.bfloat16),
            pltpu.VMEM((cuts, rows, NZ, CUT), jnp.bfloat16),
            pltpu.SemaphoreType.DMA((cuts,)),
        ],
        compiler_params=room(16),
        name="spread_step",
    )(place, *blocks)


def gram_kernel(place_ref, *refs):
    blocks, shares, (x_ref, rows_ref, band_ref) = refs[: 2 * NZ], refs[2 * NZ : 2 * NZ + 4], refs[2 * NZ + 4 :]
    along, core = place_ref[0], place_ref[2]
    for n in range(FF // CUT):
        source = (n + 2 * core) % 4
        columns = pl.ds(n * CUT, CUT)
        for half in range(2):
            packed = blocks[half * NZ : (half + 1) * NZ]
            head = jnp.stack([block[:, head_columns(source)] for block in packed])
            tail = jnp.stack([block[:, tail_columns(source)] for block in packed])
            tiles = unpack(head, tail)
            rows = jnp.concatenate(tiles, axis=1).reshape(KROWS, CUT).astype(jnp.bfloat16)
            rows_ref[pl.ds(half * KROWS, KROWS), columns] = rows
            if half == 0:
                x_ref[:, columns] = rows
    for q in range(4):
        left = rows_ref[:, pl.ds(q * QUARTER, QUARTER)]
        right = rows_ref[:, pl.ds(q * QUARTER, BAND + BLK)]
        product = lax.dot_general(
            left, right, (((0,), (0,)), ((), ())), preferred_element_type=jnp.float32
        ).astype(jnp.bfloat16)
        for sub in range(2):
            band_ref[pl.ds(q * QUARTER + sub * BLK, BLK), :] = product[
                sub * BLK : (sub + 1) * BLK, sub * BLK : sub * BLK + BAND
            ]
    terms = split_terms(largest([block[:, PACKED:] for block in blocks]))
    for d in range(4):
        shares[d][:QUARTER] = band_ref[quarter_rows(along + d), :]
        put_terms(shares[d], QUARTER, terms)


def put_terms(ref, row, terms):
    ref[pl.ds(row, EXTRA), :BLK] = terms
    ref[pl.ds(row, EXTRA), BLK:] = jnp.zeros((EXTRA, BAND - BLK), jnp.bfloat16)


def quarter_rows(q, start=0):
    return pl.ds(pl.multiple_of(start + (q % 4) * QUARTER, QUARTER), QUARTER)


def gram_band(place, blocks):
    return pl.pallas_call(
        gram_kernel,
        out_shape=[jax.ShapeDtypeStruct((QUARTER + EXTRA, BAND), jnp.bfloat16)] * 4
        + [jax.ShapeDtypeStruct((KROWS, FF), jnp.bfloat16)],
        in_specs=[SCALARS] + [MASS] * (2 * NZ),
        out_specs=[MASS] * 5,
        scratch_shapes=[
            pltpu.VMEM((2 * KROWS, FF), jnp.bfloat16),
            pltpu.VMEM((HALF, BAND), jnp.bfloat16),
        ],
        compiler_params=room(28),
        name="gram_band",
    )(place, *blocks)


def quarter_kernel(*refs):
    parts, outs = refs[:4], refs[4:]
    for half in range(2):
        rows = pl.ds(half * BLK, BLK)
        total = sum(part[rows, :].astype(jnp.float32) for part in parts)
        outs[half][:BLK] = total.astype(jnp.bfloat16)
    put_terms(outs[0], BLK, split_terms(largest([part[QUARTER:, :BLK] for part in parts])))


HALVES = [
    jax.ShapeDtypeStruct((BLK + EXTRA, BAND), jnp.bfloat16),
    jax.ShapeDtypeStruct((BLK, BAND), jnp.bfloat16),
]


def sum_quarter(parts):
    return pl.pallas_call(
        quarter_kernel,
        out_shape=HALVES,
        in_specs=[MASS] * 4,
        out_specs=[MASS] * 2,
        compiler_params=room(16),
        name="sum_quarter",
    )(*parts)


def pair_kernel(*refs):
    mine, came, outs = refs[:2], refs[2:4], refs[4:]
    for half in range(2):
        total = mine[half][:BLK].astype(jnp.float32) + came[half][:BLK].astype(jnp.float32)
        outs[half][:BLK] = total.astype(jnp.bfloat16)
    put_terms(outs[0], BLK, split_terms(largest([mine[0][BLK:, :BLK], came[0][BLK:, :BLK]])))


def add_pairs(mine, came):
    return pl.pallas_call(
        pair_kernel,
        out_shape=HALVES,
        in_specs=[MASS] * 4,
        out_specs=[MASS] * 2,
        compiler_params=room(16),
        name="add_pairs",
    )(*mine, *came)


def join_kernel(*refs):
    mine, came, (out_ref, peak_ref) = refs[:2], refs[2:4], refs[4:]
    for half in range(2):
        total = mine[half][:BLK].astype(jnp.float32) + came[half][:BLK].astype(jnp.float32)
        out_ref[pl.ds(half * BLK, BLK), :] = total.astype(jnp.bfloat16)
    peak_ref[...] = largest([mine[0][BLK:, :BLK], came[0][BLK:, :BLK]])


def join_pairs(mine, came):
    return pl.pallas_call(
        join_kernel,
        out_shape=[
            jax.ShapeDtypeStruct((QUARTER, BAND), jnp.bfloat16),
            jax.ShapeDtypeStruct((1, BLK), jnp.float32),
        ],
        in_specs=[MASS] * 4,
        out_specs=[MASS] * 2,
        compiler_params=room(16),
        name="join_pairs",
    )(*mine, *came)


def step_kernel(place_ref, x_ref, *refs):
    pieces = refs[:8]
    outs, (band_ref, gram_ref, first_ref, round_ref) = refs[8 : 8 + NZ], refs[8 + NZ :]
    core = place_ref[2]
    for side in range(2):
        for d in range(4):
            rows = quarter_rows(place_ref[side] + (4 - d), side * HALF)
            band_ref[rows, :] = pieces[side * 4 + d][...]
    for i in range(NB):
        block = band_ref[pl.ds(i * BLK, BLK), :]
        turned = block[:, BLK : BAND - BLK].T
        for d in range(NB // 2 + 1):
            j = (i + d) % NB
            gram_ref[pl.ds(i * BLK, BLK), pl.ds(j * BLK, BLK)] = block[:, d * BLK : (d + 1) * BLK]
            if 1 <= d < NB // 2:
                gram_ref[pl.ds(j * BLK, BLK), pl.ds(i * BLK, BLK)] = turned[(d - 1) * BLK : d * BLK]

    ones = jnp.ones((16, FF), jnp.bfloat16)
    bound = jnp.zeros((1, 1), jnp.float32)
    for n in range(FF // CUT):
        columns = pl.ds(n * CUT, CUT)
        gram = gram_ref[:, columns]
        first_ref[:, columns] = jnp.dot(x_ref[...], gram, preferred_element_type=jnp.float32)
        sums = jnp.dot(ones, jnp.abs(gram), preferred_element_type=jnp.float32)
        bound = jnp.maximum(bound, jnp.max(sums[:8], keepdims=True))
    inverse = 1.0 / bound
    scale = rms_match * math.sqrt(max(D, FF)) / jnp.sqrt(bound)
    for n in range(FF // CUT):
        columns = pl.ds(n * CUT, CUT)
        first = first_ref[:, columns] * inverse
        round_ref[:, columns] = first.astype(jnp.bfloat16)
        first_ref[:, columns] = linear_coef * x_ref[:, columns].astype(jnp.float32) + cubic_coef * first
    for n in range(FF // CUT):
        columns = pl.ds(n * CUT, CUT)
        second = jnp.dot(round_ref[...], gram_ref[:, columns], preferred_element_type=jnp.float32) * inverse
        step = scale * (first_ref[:, columns] + quintic_coef * second)
        step = step.reshape(NZ, PADROWS, CUT)
        head, tail = pack([step[:, 8 * t : 8 * t + 8] for t in range(4)])
        target = (n + 2 * core) % 4
        for d in range(NZ):
            outs[d][:, head_columns(target)] = head[d]
            outs[d][:, tail_columns(target)] = tail[d]


def finish(place, mine, pieces):
    return pl.pallas_call(
        step_kernel,
        out_shape=[jax.ShapeDtypeStruct((16, PACKED), jnp.bfloat16)] * NZ,
        in_specs=[SCALARS] + [MASS] * 9,
        out_specs=[MASS] * NZ,
        scratch_shapes=[
            pltpu.VMEM((FF, BAND), jnp.bfloat16),
            pltpu.VMEM((FF, FF), jnp.bfloat16),
            pltpu.VMEM((KROWS, FF), jnp.float32),
            pltpu.VMEM((KROWS, FF), jnp.bfloat16),
        ],
        compiler_params=room(40),
        name="finish",
    )(place, mine, *pieces)


def place_of(x, y, core):
    return (x * NY + y) * NC + core


def permutation(step):
    pairs = []
    for x in range(NX):
        for y in range(NY):
            for core in range(NC):
                mine = (x, y) if core == 0 else (y, x)
                to = step(*mine)
                to = to if core == 0 else to[::-1]
                pairs.append((place_of(x, y, core), place_of(*to, core)))
    return pairs


def send_along(value, by):
    return lax.ppermute(value, PLANE, permutation(lambda along, across: ((along + by) % 4, across)))


LINKS = ((1, 0, 3, 2), (3, 2, 1, 0))


def trade_across(values, first):
    links = (LINKS[first], LINKS[1 - first])
    return [
        lax.ppermute(value, PLANE, permutation(lambda along, across, link=link: (along, link[across])))
        for value, link in zip(values, links)
    ]


def collect(own, sends):
    came = {d: send_along(sends(d), d) for d in (2, 1, 3)}
    return [own, came[1], came[2], came[3]]


def swap_cores(value):
    return lax.ppermute(value, "c", [(0, 1), (1, 0)])


def trade_planes(blocks, sign):
    came = [blocks[0]] + [None] * (NZ - 1)
    for d in (4, 3, 5, 2, 6, 1, 7):
        came[d] = lax.ppermute(blocks[d], "z", [(i, (i + sign * d) % NZ) for i in range(NZ)])
    return came


def body(grads, momentum, max_logits, q_weight, k_weight):
    x, y, core = lax.axis_index("x"), lax.axis_index("y"), lax.axis_index("c")
    along, across = jnp.where(core == 0, x, y), jnp.where(core == 0, y, x)
    place = jnp.stack([along, across, core, lax.axis_index("z")]).astype(jnp.int32)
    grads, momentum = jnp.swapaxes(grads, 0, 1), jnp.swapaxes(momentum, 0, 1)
    blocks = find_direction(max_logits, grads, momentum)
    owned = trade_planes(blocks, 1)
    other = [None] * NZ
    for d in (0, 4, 3, 5, 2, 6, 1, 7):
        other[d] = swap_cores(owned[d])
    *shares, mine = gram_band(place, owned + other)
    shares[0], grads_again, momentum = lax.optimization_barrier((shares[0], grads, momentum))
    parts = collect(shares[0], lambda d: shares[d])
    new_momentum = add_momentum(grads_again, momentum)
    parts[0], new_momentum = lax.optimization_barrier((parts[0], new_momentum))
    held = sum_quarter(parts)
    held = add_pairs(held, trade_across(held, 0))
    held, peak = join_pairs(held, trade_across(held, 1))
    pieces = collect(held, lambda d: held)
    pieces[0], pieces[2] = lax.optimization_barrier((pieces[0], pieces[2]))
    other = [swap_cores(piece) for piece in pieces]
    step = list(finish(place, mine, pieces + other))
    step[0], peak, q_weight, k_weight = lax.optimization_barrier((step[0], peak, q_weight, k_weight))
    step = trade_planes(step, -1)
    peak = peak[0, : max_logits.shape[1]]

    gamma = jnp.minimum(1.0, clip_limit / peak)
    root = jnp.sqrt(gamma)
    local_heads = k_weight.shape[1] // NOPE
    first_head = lax.axis_index("z") * local_heads
    gamma_mine = lax.dynamic_slice_in_dim(gamma, first_head, local_heads)
    root_mine = lax.dynamic_slice_in_dim(root, first_head, local_heads)
    q_factor = jnp.concatenate(
        [
            jnp.broadcast_to(root_mine[:, None], (local_heads, NOPE)),
            jnp.broadcast_to(gamma_mine[:, None], (local_heads, ROPE)),
        ],
        axis=1,
    )
    q_view = q_weight.reshape(q_weight.shape[0], local_heads, NOPE + ROPE).astype(jnp.float32)
    q_clipped = (q_view * q_factor[None]).astype(jnp.bfloat16).reshape(q_weight.shape)
    k_view = k_weight.reshape(k_weight.shape[0], local_heads, NOPE).astype(jnp.float32)
    k_clipped = (k_view * root_mine[None, :, None]).astype(jnp.bfloat16).reshape(k_weight.shape)
    step[0], q_clipped, k_clipped = lax.optimization_barrier((step[0], q_clipped, k_clipped))
    step = jnp.swapaxes(spread_step(place, step, grads.shape[0]), 0, 1)
    new_momentum = jnp.swapaxes(new_momentum, 0, 1)
    return (new_momentum, step, q_clipped, k_clipped)


def solution(mesh):
    split = Mesh(mesh.devices.reshape(NX, NY, NC, NZ), ("x", "y", "c", "z"))
    rows = P(None, ("x", "y", "c", "z"), None)
    heads = P(("x", "y", "c"), "z")
    return jax.shard_map(
        body,
        mesh=split,
        in_specs=(rows, rows, P(("x", "y", "c", "z"), None), heads, heads),
        out_specs=(rows, rows, heads, heads),
        check_vma=False,
    )
```

```python
import math

import jax
import jax.numpy as jnp
from jax import lax
from jax.experimental import pallas as pl
from jax.experimental.pallas import tpu as pltpu
from jax.sharding import Mesh, PartitionSpec as P

D = 7168
FF = 2048
NOPE = 128
ROPE = 64

decay_rate = 0.9
linear_coef = 3.4445
cubic_coef = -4.775
quintic_coef = 2.0315
clip_limit = 100.0
rms_match = 0.2

NX, NY, NC, NZ = 4, 4, 2, 8
PLANE = ("x", "y", "c")
BLK = 128
NB = FF // BLK
HALF = FF // 2
BAND = (NB // 2 + 1) * BLK
PADROWS = 32
KROWS = NZ * PADROWS
CUT = 512
TAIL = 384
PACKED = FF + (FF // CUT) * TAIL
WIDTH = PACKED + BLK
EXTRA = 16
QUARTER = 2 * BLK

MASS = pl.BlockSpec(memory_space=pltpu.VMEM)
FAR = pl.BlockSpec(memory_space=pl.ANY)


def own_place():
    x, y, core = lax.axis_index("x"), lax.axis_index("y"), lax.axis_index("c")
    return jnp.where(core == 0, x, y), jnp.where(core == 0, y, x), core


def room(mib):
    return pltpu.CompilerParams(vmem_limit_bytes=mib * 1024 * 1024)


def low_rows(value):
    return lax.broadcasted_iota(jnp.int32, value.shape, 1) < 4


def pack(tiles):
    t0, t1, t2, t3 = tiles
    e2, e3 = t2[:, :, TAIL:], t3[:, :, TAIL:]
    moved = jnp.concatenate([pltpu.roll(e2, 4, 1), e2, pltpu.roll(e3, 4, 1)], axis=2)
    last = t3[:, :, :TAIL]
    last = jnp.where(low_rows(last), last, moved)
    head = jnp.concatenate([t0, t1], axis=1)
    tail = jnp.concatenate([t2[:, :, :TAIL], last], axis=1)
    return head.astype(jnp.bfloat16), tail.astype(jnp.bfloat16)


def unpack(head, tail):
    head, tail = head.astype(jnp.float32), tail.astype(jnp.float32)
    t2, last = tail[:, :8], tail[:, 8:]
    m0, m1, m2 = last[:, :, :BLK], last[:, :, BLK : 2 * BLK], last[:, :, 2 * BLK :]
    e2 = jnp.where(low_rows(m0), pltpu.roll(m0, 4, 1), m1)
    e3 = pltpu.roll(m2, 4, 1)
    t2 = jnp.concatenate([t2, e2], axis=2)
    t3 = jnp.concatenate([last, e3], axis=2)
    t3 = jnp.where(low_rows(t3), t3, 0.0)
    return head[:, :8], head[:, 8:], t2, t3


def split_terms(value):
    high = value.astype(jnp.bfloat16).astype(jnp.float32)
    rest = value - high
    middle = rest.astype(jnp.bfloat16).astype(jnp.float32)
    row = lax.broadcasted_iota(jnp.int32, (EXTRA, BLK), 0)
    tile = jnp.where(row == 0, high, jnp.where(row == 1, middle, jnp.where(row == 2, rest - middle, 0.0)))
    return tile.astype(jnp.bfloat16)


def largest(tiles):
    best = None
    for tile in tiles:
        tile = tile.astype(jnp.float32)
        value = tile[0:1] + tile[1:2] + tile[2:3]
        best = value if best is None else jnp.maximum(best, value)
    return best


def head_columns(n):
    return pl.ds(pl.multiple_of(n * CUT, CUT), CUT)


def tail_columns(n):
    return pl.ds(pl.multiple_of(FF + n * TAIL, BLK), TAIL)


def direction_kernel(logits_ref, grads_ref, momentum_ref, *refs):
    outs, (grads_buf, momentum_buf, packed_ref, grads_sem, momentum_sem) = refs[:NZ], refs[NZ:]
    z = lax.axis_index("z")
    copies = []
    for n in range(FF // CUT):
        columns = pl.ds(n * CUT, CUT)
        pair = (
            pltpu.make_async_copy(momentum_ref.at[:, :, columns], momentum_buf.at[n], momentum_sem.at[n]),
            pltpu.make_async_copy(grads_ref.at[:, :, columns], grads_buf.at[n], grads_sem.at[n]),
        )
        for copy in pair:
            copy.start()
        copies.append(pair)
    for n in range(FF // CUT):
        for copy in copies[n]:
            copy.wait()
        grads = grads_buf[n].astype(jnp.float32)
        direction = grads + decay_rate * (decay_rate * momentum_buf[n] + grads)
        rows, mats, columns = direction.shape
        direction = jnp.concatenate([direction, jnp.zeros((PADROWS - rows, mats, columns), jnp.float32)], axis=0)
        head, tail = pack([jnp.swapaxes(direction[8 * t : 8 * t + 8], 0, 1) for t in range(4)])
        packed_ref[:, :, head_columns(n)] = head
        packed_ref[:, :, tail_columns(n)] = tail
    logits = logits_ref[...]
    terms = split_terms(jnp.concatenate([logits, jnp.zeros((1, BLK - logits.shape[1]), jnp.float32)], axis=1))
    for d in range(NZ):
        outs[d][:, :PACKED] = packed_ref[(z + d) % NZ]
        outs[d][:, PACKED:] = terms


def find_direction(logits, grads, momentum):
    rows, mats = grads.shape[:2]
    cuts = FF // CUT
    return pl.pallas_call(
        direction_kernel,
        out_shape=[jax.ShapeDtypeStruct((16, WIDTH), jnp.bfloat16)] * NZ,
        in_specs=[MASS] + [FAR] * 2,
        out_specs=[MASS] * NZ,
        scratch_shapes=[
            pltpu.VMEM((cuts, rows, mats, CUT), jnp.bfloat16),
            pltpu.VMEM((cuts, rows, mats, CUT), jnp.float32),
            pltpu.VMEM((mats, 16, PACKED), jnp.bfloat16),
            pltpu.SemaphoreType.DMA((cuts,)),
            pltpu.SemaphoreType.DMA((cuts,)),
        ],
        compiler_params=room(53),
        name="find_direction",
    )(logits, grads, momentum)


def momentum_kernel(grads_ref, momentum_ref, out_ref, grads_buf, momentum_buf, in_sem, out_sem):
    copies = []
    for n in range(FF // CUT):
        columns = pl.ds(n * CUT, CUT)
        trio = (
            pltpu.make_async_copy(momentum_ref.at[:, :, columns], momentum_buf.at[n], in_sem.at[0, n]),
            pltpu.make_async_copy(grads_ref.at[:, :, columns], grads_buf.at[n], in_sem.at[1, n]),
            pltpu.make_async_copy(momentum_buf.at[n], out_ref.at[:, :, columns], out_sem.at[n]),
        )
        trio[0].start()
        trio[1].start()
        copies.append(trio)
    for n in range(FF // CUT):
        copies[n][0].wait()
        copies[n][1].wait()
        momentum_buf[n] = decay_rate * momentum_buf[n] + grads_buf[n].astype(jnp.float32)
        copies[n][2].start()
    for trio in copies:
        trio[2].wait()


def add_momentum(grads, momentum):
    rows, mats = grads.shape[:2]
    cuts = FF // CUT
    return pl.pallas_call(
        momentum_kernel,
        out_shape=jax.ShapeDtypeStruct(grads.shape, jnp.float32),
        in_specs=[FAR] * 2,
        out_specs=FAR,
        scratch_shapes=[
            pltpu.VMEM((cuts, rows, mats, CUT), jnp.bfloat16),
            pltpu.VMEM((cuts, rows, mats, CUT), jnp.float32),
            pltpu.SemaphoreType.DMA((2, cuts)),
            pltpu.SemaphoreType.DMA((cuts,)),
        ],
        compiler_params=room(53),
        name="add_momentum",
    )(grads, momentum)


def spread_kernel(*refs):
    blocks, (out_ref, packed_ref, rows_ref, sem) = refs[:NZ], refs[NZ:]
    z = lax.axis_index("z")
    for d in range(NZ):
        packed_ref[(z + d) % NZ] = blocks[d][...]
    copies = []
    for n in range(FF // CUT):
        tiles = unpack(packed_ref[:, :, head_columns(n)], packed_ref[:, :, tail_columns(n)])
        rows = jnp.concatenate([jnp.swapaxes(t, 0, 1) for t in tiles], axis=0)
        rows_ref[n] = rows[: out_ref.shape[0]].astype(jnp.bfloat16)
        copy = pltpu.make_async_copy(rows_ref.at[n], out_ref.at[:, :, pl.ds(n * CUT, CUT)], sem.at[n])
        copy.start()
        copies.append(copy)
    for copy in copies:
        copy.wait()


def spread_step(blocks, rows):
    cuts = FF // CUT
    return pl.pallas_call(
        spread_kernel,
        out_shape=jax.ShapeDtypeStruct((rows, NZ, FF), jnp.bfloat16),
        in_specs=[MASS] * NZ,
        out_specs=pl.BlockSpec(memory_space=pl.ANY),
        scratch_shapes=[
            pltpu.VMEM((NZ, 16, PACKED), jnp.bfloat16),
            pltpu.VMEM((cuts, rows, NZ, CUT), jnp.bfloat16),
            pltpu.SemaphoreType.DMA((cuts,)),
        ],
        compiler_params=room(16),
        name="spread_step",
    )(*blocks)


def gram_kernel(*refs):
    blocks, shares, (x_ref, rows_ref, band_ref) = refs[: 2 * NZ], refs[2 * NZ : 2 * NZ + 4], refs[2 * NZ + 4 :]
    along, _, core = own_place()
    for n in range(FF // CUT):
        source = (n + 2 * core) % 4
        columns = pl.ds(n * CUT, CUT)
        for half in range(2):
            packed = blocks[half * NZ : (half + 1) * NZ]
            head = jnp.stack([block[:, head_columns(source)] for block in packed])
            tail = jnp.stack([block[:, tail_columns(source)] for block in packed])
            tiles = unpack(head, tail)
            rows = jnp.concatenate(tiles, axis=1).reshape(KROWS, CUT).astype(jnp.bfloat16)
            rows_ref[pl.ds(half * KROWS, KROWS), columns] = rows
            if half == 0:
                x_ref[:, columns] = rows
    for q in range(4):
        left = rows_ref[:, pl.ds(q * QUARTER, QUARTER)]
        right = rows_ref[:, pl.ds(q * QUARTER, BAND + BLK)]
        product = lax.dot_general(
            left, right, (((0,), (0,)), ((), ())), preferred_element_type=jnp.float32
        ).astype(jnp.bfloat16)
        for sub in range(2):
            band_ref[pl.ds(q * QUARTER + sub * BLK, BLK), :] = product[
                sub * BLK : (sub + 1) * BLK, sub * BLK : sub * BLK + BAND
            ]
    terms = split_terms(largest([block[:, PACKED:] for block in blocks]))
    for d in range(4):
        shares[d][:QUARTER] = band_ref[quarter_rows(along + d), :]
        put_terms(shares[d], QUARTER, terms)


def put_terms(ref, row, terms):
    ref[pl.ds(row, EXTRA), :BLK] = terms
    ref[pl.ds(row, EXTRA), BLK:] = jnp.zeros((EXTRA, BAND - BLK), jnp.bfloat16)


def quarter_rows(q, start=0):
    return pl.ds(pl.multiple_of(start + (q % 4) * QUARTER, QUARTER), QUARTER)


def gram_band(blocks):
    return pl.pallas_call(
        gram_kernel,
        out_shape=[jax.ShapeDtypeStruct((QUARTER + EXTRA, BAND), jnp.bfloat16)] * 4
        + [jax.ShapeDtypeStruct((KROWS, FF), jnp.bfloat16)],
        in_specs=[MASS] * (2 * NZ),
        out_specs=[MASS] * 5,
        scratch_shapes=[
            pltpu.VMEM((2 * KROWS, FF), jnp.bfloat16),
            pltpu.VMEM((HALF, BAND), jnp.bfloat16),
        ],
        compiler_params=room(28),
        name="gram_band",
    )(*blocks)


def quarter_kernel(*refs):
    parts, outs = refs[:4], refs[4:]
    for half in range(2):
        rows = pl.ds(half * BLK, BLK)
        total = sum(part[rows, :].astype(jnp.float32) for part in parts)
        outs[half][:BLK] = total.astype(jnp.bfloat16)
    put_terms(outs[0], BLK, split_terms(largest([part[QUARTER:, :BLK] for part in parts])))


HALVES = [
    jax.ShapeDtypeStruct((BLK + EXTRA, BAND), jnp.bfloat16),
    jax.ShapeDtypeStruct((BLK, BAND), jnp.bfloat16),
]


def sum_quarter(parts):
    return pl.pallas_call(
        quarter_kernel,
        out_shape=HALVES,
        in_specs=[MASS] * 4,
        out_specs=[MASS] * 2,
        compiler_params=room(16),
        name="sum_quarter",
    )(*parts)


def pair_kernel(*refs):
    mine, came, outs = refs[:2], refs[2:4], refs[4:]
    for half in range(2):
        total = mine[half][:BLK].astype(jnp.float32) + came[half][:BLK].astype(jnp.float32)
        outs[half][:BLK] = total.astype(jnp.bfloat16)
    put_terms(outs[0], BLK, split_terms(largest([mine[0][BLK:, :BLK], came[0][BLK:, :BLK]])))


def add_pairs(mine, came):
    return pl.pallas_call(
        pair_kernel,
        out_shape=HALVES,
        in_specs=[MASS] * 4,
        out_specs=[MASS] * 2,
        compiler_params=room(16),
        name="add_pairs",
    )(*mine, *came)


def join_kernel(*refs):
    mine, came, (out_ref, peak_ref) = refs[:2], refs[2:4], refs[4:]
    for half in range(2):
        total = mine[half][:BLK].astype(jnp.float32) + came[half][:BLK].astype(jnp.float32)
        out_ref[pl.ds(half * BLK, BLK), :] = total.astype(jnp.bfloat16)
    peak_ref[...] = largest([mine[0][BLK:, :BLK], came[0][BLK:, :BLK]])


def join_pairs(mine, came):
    return pl.pallas_call(
        join_kernel,
        out_shape=[
            jax.ShapeDtypeStruct((QUARTER, BAND), jnp.bfloat16),
            jax.ShapeDtypeStruct((1, BLK), jnp.float32),
        ],
        in_specs=[MASS] * 4,
        out_specs=[MASS] * 2,
        compiler_params=room(16),
        name="join_pairs",
    )(*mine, *came)


def step_kernel(x_ref, *refs):
    pieces = refs[:8]
    outs, (band_ref, gram_ref, first_ref, round_ref) = refs[8 : 8 + NZ], refs[8 + NZ :]
    *places, core = own_place()
    for side in range(2):
        for d in range(4):
            rows = quarter_rows(places[side] + (4 - d), side * HALF)
            band_ref[rows, :] = pieces[side * 4 + d][...]
    for i in range(NB):
        block = band_ref[pl.ds(i * BLK, BLK), :]
        turned = block[:, BLK : BAND - BLK].T
        for d in range(NB // 2 + 1):
            j = (i + d) % NB
            gram_ref[pl.ds(i * BLK, BLK), pl.ds(j * BLK, BLK)] = block[:, d * BLK : (d + 1) * BLK]
            if 1 <= d < NB // 2:
                gram_ref[pl.ds(j * BLK, BLK), pl.ds(i * BLK, BLK)] = turned[(d - 1) * BLK : d * BLK]

    ones = jnp.ones((16, FF), jnp.bfloat16)
    bound = jnp.zeros((1, 1), jnp.float32)
    for n in range(FF // CUT):
        columns = pl.ds(n * CUT, CUT)
        gram = gram_ref[:, columns]
        first_ref[:, columns] = jnp.dot(x_ref[...], gram, preferred_element_type=jnp.float32)
        sums = jnp.dot(ones, jnp.abs(gram), preferred_element_type=jnp.float32)
        bound = jnp.maximum(bound, jnp.max(sums[:8], keepdims=True))
    inverse = 1.0 / bound
    scale = rms_match * math.sqrt(max(D, FF)) / jnp.sqrt(bound)
    for n in range(FF // CUT):
        columns = pl.ds(n * CUT, CUT)
        first = first_ref[:, columns] * inverse
        round_ref[:, columns] = first.astype(jnp.bfloat16)
        first_ref[:, columns] = linear_coef * x_ref[:, columns].astype(jnp.float32) + cubic_coef * first
    for n in range(FF // CUT):
        columns = pl.ds(n * CUT, CUT)
        second = jnp.dot(round_ref[...], gram_ref[:, columns], preferred_element_type=jnp.float32) * inverse
        step = scale * (first_ref[:, columns] + quintic_coef * second)
        step = step.reshape(NZ, PADROWS, CUT)
        head, tail = pack([step[:, 8 * t : 8 * t + 8] for t in range(4)])
        target = (n + 2 * core) % 4
        for d in range(NZ):
            outs[d][:, head_columns(target)] = head[d]
            outs[d][:, tail_columns(target)] = tail[d]


def finish(mine, pieces):
    return pl.pallas_call(
        step_kernel,
        out_shape=[jax.ShapeDtypeStruct((16, PACKED), jnp.bfloat16)] * NZ,
        in_specs=[MASS] * 9,
        out_specs=[MASS] * NZ,
        scratch_shapes=[
            pltpu.VMEM((FF, BAND), jnp.bfloat16),
            pltpu.VMEM((FF, FF), jnp.bfloat16),
            pltpu.VMEM((KROWS, FF), jnp.float32),
            pltpu.VMEM((KROWS, FF), jnp.bfloat16),
        ],
        compiler_params=room(28),
        name="finish",
    )(mine, *pieces)


def clip_kernel(peak_ref, q_ref, k_ref, q_out, k_out):
    z = lax.axis_index("z")
    gamma = jnp.minimum(1.0, clip_limit / peak_ref[...])
    square = (BLK, BLK)
    diagonal = lax.broadcasted_iota(jnp.int32, square, 0) == lax.broadcasted_iota(jnp.int32, square, 1)
    gamma = jnp.sum(jnp.where(diagonal, jnp.broadcast_to(gamma, square), 0.0), axis=1, keepdims=True)
    root = jnp.sqrt(gamma)
    for source, out, width in ((q_ref, q_out, NOPE + ROPE), (k_ref, k_out, NOPE)):
        columns = source.shape[1]
        column = lax.broadcasted_iota(jnp.int32, (BLK, columns), 1)
        head = column // width
        chosen = lax.broadcasted_iota(jnp.int32, (BLK, columns), 0) == head + z * (columns // width)
        value = jnp.where(column - head * width < NOPE, root, gamma)
        factor = jnp.sum(jnp.where(chosen, value, 0.0), axis=0, keepdims=True)
        out[...] = (source[...].astype(jnp.float32) * factor).astype(jnp.bfloat16)


def clip(peak, q_weight, k_weight):
    return pl.pallas_call(
        clip_kernel,
        out_shape=[jax.ShapeDtypeStruct(weight.shape, jnp.bfloat16) for weight in (q_weight, k_weight)],
        in_specs=[MASS] * 3,
        out_specs=[MASS] * 2,
        compiler_params=room(16),
        name="clip",
    )(peak, q_weight, k_weight)


def place_of(x, y, core):
    return (x * NY + y) * NC + core


def permutation(step):
    pairs = []
    for x in range(NX):
        for y in range(NY):
            for core in range(NC):
                mine = (x, y) if core == 0 else (y, x)
                to = step(*mine)
                to = to if core == 0 else to[::-1]
                pairs.append((place_of(x, y, core), place_of(*to, core)))
    return pairs


def send_along(value, by):
    return lax.ppermute(value, PLANE, permutation(lambda along, across: ((along + by) % 4, across)))


LINKS = ((1, 0, 3, 2), (3, 2, 1, 0))


def trade_across(values, first):
    links = (LINKS[first], LINKS[1 - first])
    return [
        lax.ppermute(value, PLANE, permutation(lambda along, across, link=link: (along, link[across])))
        for value, link in zip(values, links)
    ]


def collect(own, sends, order):
    came = {d: send_along(sends(d), d) for d in order}
    return [own, came[1], came[2], came[3]]


def swap_cores(value):
    return lax.ppermute(value, "c", [(0, 1), (1, 0)])


def trade_planes(blocks, sign):
    came = [blocks[0]] + [None] * (NZ - 1)
    for d in (4, 3, 5, 2, 6, 1, 7):
        came[d] = lax.ppermute(blocks[d], "z", [(i, (i + sign * d) % NZ) for i in range(NZ)])
    return came


def body(grads, momentum, max_logits, q_weight, k_weight):
    grads, momentum = jnp.swapaxes(grads, 0, 1), jnp.swapaxes(momentum, 0, 1)
    blocks = find_direction(max_logits, grads, momentum)
    owned = trade_planes(blocks, 1)
    other = [None] * NZ
    for d in (0, 4, 3, 5, 2, 6, 1, 7):
        other[d] = swap_cores(owned[d])
    *shares, mine = gram_band(owned + other)
    shares[0], grads_again, momentum = lax.optimization_barrier((shares[0], grads, momentum))
    parts = collect(shares[0], lambda d: shares[d], (2, 1, 3))
    new_momentum = add_momentum(grads_again, momentum)
    parts[0], new_momentum = lax.optimization_barrier((parts[0], new_momentum))
    held = sum_quarter(parts)
    held = add_pairs(held, trade_across(held, 0))
    held, peak = join_pairs(held, trade_across(held, 1))
    pieces = collect(held, lambda d: held, (1, 3, 2))
    q_clipped, k_clipped = clip(peak, q_weight, k_weight)
    pieces[0], pieces[1], q_clipped, k_clipped = lax.optimization_barrier((pieces[0], pieces[1], q_clipped, k_clipped))
    other = [swap_cores(piece) for piece in pieces]
    step = finish(mine, pieces + other)
    step = trade_planes(step, -1)
    step = jnp.swapaxes(spread_step(step, grads.shape[0]), 0, 1)
    return (jnp.swapaxes(new_momentum, 0, 1), step, q_clipped, k_clipped)


def solution(mesh):
    split = Mesh(mesh.devices.reshape(NX, NY, NC, NZ), ("x", "y", "c", "z"))
    rows = P(None, ("x", "y", "c", "z"), None)
    heads = P(("x", "y", "c"), "z")
    return jax.shard_map(
        body,
        mesh=split,
        in_specs=(rows, rows, P(("x", "y", "c", "z"), None), heads, heads),
        out_specs=(rows, rows, heads, heads),
        check_vma=False,
    )
```

```python
import math

import jax
import jax.numpy as jnp
from jax import lax
from jax.experimental import pallas as pl
from jax.experimental.pallas import tpu as pltpu
from jax.sharding import Mesh, PartitionSpec as P

D = 7168
FF = 2048
NOPE = 128
ROPE = 64

decay_rate = 0.9
linear_coef = 3.4445
cubic_coef = -4.775
quintic_coef = 2.0315
clip_limit = 100.0
rms_match = 0.2

NX, NY, NC, NZ = 4, 4, 2, 8
PLANE = ("x", "y", "c")
BLK = 128
NB = FF // BLK
HALF = FF // 2
BAND = (NB // 2 + 1) * BLK
PADROWS = 32
KROWS = NZ * PADROWS
CUT = 512
TAIL = 384
PACKED = FF + (FF // CUT) * TAIL
WIDTH = PACKED + BLK
EXTRA = 16
QUARTER = 2 * BLK

MASS = pl.BlockSpec(memory_space=pltpu.VMEM)
FAR = pl.BlockSpec(memory_space=pl.ANY)


def own_place():
    x, y, core = lax.axis_index("x"), lax.axis_index("y"), lax.axis_index("c")
    return jnp.where(core == 0, x, y), jnp.where(core == 0, y, x), core


def room(mib):
    return pltpu.CompilerParams(vmem_limit_bytes=mib * 1024 * 1024)


def low_rows(value):
    return lax.broadcasted_iota(jnp.int32, value.shape, 1) < 4


def pack(tiles):
    t0, t1, t2, t3 = tiles
    e2, e3 = t2[:, :, TAIL:], t3[:, :, TAIL:]
    moved = jnp.concatenate([pltpu.roll(e2, 4, 1), e2, pltpu.roll(e3, 4, 1)], axis=2)
    last = t3[:, :, :TAIL]
    last = jnp.where(low_rows(last), last, moved)
    head = jnp.concatenate([t0, t1], axis=1)
    tail = jnp.concatenate([t2[:, :, :TAIL], last], axis=1)
    return head.astype(jnp.bfloat16), tail.astype(jnp.bfloat16)


def unpack(head, tail):
    head, tail = head.astype(jnp.float32), tail.astype(jnp.float32)
    t2, last = tail[:, :8], tail[:, 8:]
    m0, m1, m2 = last[:, :, :BLK], last[:, :, BLK : 2 * BLK], last[:, :, 2 * BLK :]
    e2 = jnp.where(low_rows(m0), pltpu.roll(m0, 4, 1), m1)
    e3 = pltpu.roll(m2, 4, 1)
    t2 = jnp.concatenate([t2, e2], axis=2)
    t3 = jnp.concatenate([last, e3], axis=2)
    t3 = jnp.where(low_rows(t3), t3, 0.0)
    return head[:, :8], head[:, 8:], t2, t3


def split_terms(value):
    high = value.astype(jnp.bfloat16).astype(jnp.float32)
    rest = value - high
    middle = rest.astype(jnp.bfloat16).astype(jnp.float32)
    row = lax.broadcasted_iota(jnp.int32, (EXTRA, BLK), 0)
    tile = jnp.where(row == 0, high, jnp.where(row == 1, middle, jnp.where(row == 2, rest - middle, 0.0)))
    return tile.astype(jnp.bfloat16)


def largest(tiles):
    best = None
    for tile in tiles:
        tile = tile.astype(jnp.float32)
        value = tile[0:1] + tile[1:2] + tile[2:3]
        best = value if best is None else jnp.maximum(best, value)
    return best


def head_columns(n):
    return pl.ds(pl.multiple_of(n * CUT, CUT), CUT)


def tail_columns(n):
    return pl.ds(pl.multiple_of(FF + n * TAIL, BLK), TAIL)


def direction_kernel(logits_ref, grads_ref, momentum_ref, *refs):
    outs, (grads_buf, momentum_buf, packed_ref, logits_buf, grads_sem, momentum_sem, logits_sem) = refs[:NZ], refs[NZ:]
    z = lax.axis_index("z")
    logits_copy = pltpu.make_async_copy(logits_ref, logits_buf, logits_sem)
    logits_copy.start()
    copies = []
    for n in range(FF // CUT):
        columns = pl.ds(n * CUT, CUT)
        pair = (
            pltpu.make_async_copy(momentum_ref.at[:, :, columns], momentum_buf.at[n], momentum_sem.at[n]),
            pltpu.make_async_copy(grads_ref.at[:, :, columns], grads_buf.at[n], grads_sem.at[n]),
        )
        for copy in pair:
            copy.start()
        copies.append(pair)
    for n in range(FF // CUT):
        for copy in copies[n]:
            copy.wait()
        grads = grads_buf[n].astype(jnp.float32)
        direction = grads + decay_rate * (decay_rate * momentum_buf[n] + grads)
        rows, mats, columns = direction.shape
        direction = jnp.concatenate([direction, jnp.zeros((PADROWS - rows, mats, columns), jnp.float32)], axis=0)
        head, tail = pack([jnp.swapaxes(direction[8 * t : 8 * t + 8], 0, 1) for t in range(4)])
        packed_ref[:, :, head_columns(n)] = head
        packed_ref[:, :, tail_columns(n)] = tail
    logits_copy.wait()
    logits = logits_buf[...]
    terms = split_terms(jnp.concatenate([logits, jnp.zeros((1, BLK - logits.shape[1]), jnp.float32)], axis=1))
    for d in range(NZ):
        outs[d][:, :PACKED] = packed_ref[(z + d) % NZ]
        outs[d][:, PACKED:] = terms


def find_direction(logits, grads, momentum):
    rows, mats = grads.shape[:2]
    cuts = FF // CUT
    return pl.pallas_call(
        direction_kernel,
        out_shape=[jax.ShapeDtypeStruct((16, WIDTH), jnp.bfloat16)] * NZ,
        in_specs=[FAR] * 3,
        out_specs=[MASS] * NZ,
        scratch_shapes=[
            pltpu.VMEM((cuts, rows, mats, CUT), jnp.bfloat16),
            pltpu.VMEM((cuts, rows, mats, CUT), jnp.float32),
            pltpu.VMEM((mats, 16, PACKED), jnp.bfloat16),
            pltpu.VMEM(logits.shape, jnp.float32),
            pltpu.SemaphoreType.DMA((cuts,)),
            pltpu.SemaphoreType.DMA((cuts,)),
            pltpu.SemaphoreType.DMA(()),
        ],
        compiler_params=room(53),
        name="find_direction",
    )(logits, grads, momentum)


def momentum_kernel(grads_ref, momentum_ref, out_ref, grads_buf, momentum_buf, in_sem, out_sem):
    copies = []
    for n in range(FF // CUT):
        columns = pl.ds(n * CUT, CUT)
        trio = (
            pltpu.make_async_copy(momentum_ref.at[:, :, columns], momentum_buf.at[n], in_sem.at[0, n]),
            pltpu.make_async_copy(grads_ref.at[:, :, columns], grads_buf.at[n], in_sem.at[1, n]),
            pltpu.make_async_copy(momentum_buf.at[n], out_ref.at[:, :, columns], out_sem.at[n]),
        )
        trio[0].start()
        trio[1].start()
        copies.append(trio)
    for n in range(FF // CUT):
        copies[n][0].wait()
        copies[n][1].wait()
        momentum_buf[n] = decay_rate * momentum_buf[n] + grads_buf[n].astype(jnp.float32)
        copies[n][2].start()
    for trio in copies:
        trio[2].wait()


def add_momentum(grads, momentum):
    rows, mats = grads.shape[:2]
    cuts = FF // CUT
    return pl.pallas_call(
        momentum_kernel,
        out_shape=jax.ShapeDtypeStruct(grads.shape, jnp.float32),
        in_specs=[FAR] * 2,
        out_specs=FAR,
        scratch_shapes=[
            pltpu.VMEM((cuts, rows, mats, CUT), jnp.bfloat16),
            pltpu.VMEM((cuts, rows, mats, CUT), jnp.float32),
            pltpu.SemaphoreType.DMA((2, cuts)),
            pltpu.SemaphoreType.DMA((cuts,)),
        ],
        compiler_params=room(55),
        name="add_momentum",
    )(grads, momentum)


def spread_kernel(*refs):
    blocks, (out_ref, packed_ref, rows_ref, sem) = refs[:NZ], refs[NZ:]
    z = lax.axis_index("z")
    for d in range(NZ):
        packed_ref[(z + d) % NZ] = blocks[d][...]
    copies = []
    for n in range(FF // CUT):
        tiles = unpack(packed_ref[:, :, head_columns(n)], packed_ref[:, :, tail_columns(n)])
        rows = jnp.concatenate([jnp.swapaxes(t, 0, 1) for t in tiles], axis=0)
        rows_ref[n] = rows[: out_ref.shape[0]].astype(jnp.bfloat16)
        copy = pltpu.make_async_copy(rows_ref.at[n], out_ref.at[:, :, pl.ds(n * CUT, CUT)], sem.at[n])
        copy.start()
        copies.append(copy)
    for copy in copies:
        copy.wait()


def spread_step(blocks, rows):
    cuts = FF // CUT
    return pl.pallas_call(
        spread_kernel,
        out_shape=jax.ShapeDtypeStruct((rows, NZ, FF), jnp.bfloat16),
        in_specs=[MASS] * NZ,
        out_specs=pl.BlockSpec(memory_space=pl.ANY),
        scratch_shapes=[
            pltpu.VMEM((NZ, 16, PACKED), jnp.bfloat16),
            pltpu.VMEM((cuts, rows, NZ, CUT), jnp.bfloat16),
            pltpu.SemaphoreType.DMA((cuts,)),
        ],
        compiler_params=room(16),
        name="spread_step",
    )(*blocks)


def gram_kernel(*refs):
    blocks, shares, (x_ref, rows_ref, band_ref) = refs[: 2 * NZ], refs[2 * NZ : 2 * NZ + 4], refs[2 * NZ + 4 :]
    along, _, core = own_place()
    for n in range(FF // CUT):
        source = (n + 2 * core) % 4
        columns = pl.ds(n * CUT, CUT)
        for half in range(2):
            packed = blocks[half * NZ : (half + 1) * NZ]
            head = jnp.stack([block[:, head_columns(source)] for block in packed])
            tail = jnp.stack([block[:, tail_columns(source)] for block in packed])
            tiles = unpack(head, tail)
            rows = jnp.concatenate(tiles, axis=1).reshape(KROWS, CUT).astype(jnp.bfloat16)
            rows_ref[pl.ds(half * KROWS, KROWS), columns] = rows
            if half == 0:
                x_ref[:, columns] = rows
    for q in range(4):
        left = rows_ref[:, pl.ds(q * QUARTER, QUARTER)]
        right = rows_ref[:, pl.ds(q * QUARTER, BAND + BLK)]
        product = lax.dot_general(
            left, right, (((0,), (0,)), ((), ())), preferred_element_type=jnp.float32
        ).astype(jnp.bfloat16)
        for sub in range(2):
            band_ref[pl.ds(q * QUARTER + sub * BLK, BLK), :] = product[
                sub * BLK : (sub + 1) * BLK, sub * BLK : sub * BLK + BAND
            ]
    terms = split_terms(largest([block[:, PACKED:] for block in blocks]))
    for d in range(4):
        shares[d][:QUARTER] = band_ref[quarter_rows(along + d), :]
        put_terms(shares[d], QUARTER, terms)


def put_terms(ref, row, terms):
    ref[pl.ds(row, EXTRA), :BLK] = terms
    ref[pl.ds(row, EXTRA), BLK:] = jnp.zeros((EXTRA, BAND - BLK), jnp.bfloat16)


def quarter_rows(q, start=0):
    return pl.ds(pl.multiple_of(start + (q % 4) * QUARTER, QUARTER), QUARTER)


def gram_band(blocks):
    return pl.pallas_call(
        gram_kernel,
        out_shape=[jax.ShapeDtypeStruct((QUARTER + EXTRA, BAND), jnp.bfloat16)] * 4
        + [jax.ShapeDtypeStruct((KROWS, FF), jnp.bfloat16)],
        in_specs=[MASS] * (2 * NZ),
        out_specs=[MASS] * 5,
        scratch_shapes=[
            pltpu.VMEM((2 * KROWS, FF), jnp.bfloat16),
            pltpu.VMEM((HALF, BAND), jnp.bfloat16),
        ],
        compiler_params=room(28),
        name="gram_band",
    )(*blocks)


def quarter_kernel(*refs):
    parts, outs = refs[:4], refs[4:]
    for half in range(2):
        rows = pl.ds(half * BLK, BLK)
        total = sum(part[rows, :].astype(jnp.float32) for part in parts)
        outs[half][:BLK] = total.astype(jnp.bfloat16)
    put_terms(outs[0], BLK, split_terms(largest([part[QUARTER:, :BLK] for part in parts])))


HALVES = [
    jax.ShapeDtypeStruct((BLK + EXTRA, BAND), jnp.bfloat16),
    jax.ShapeDtypeStruct((BLK, BAND), jnp.bfloat16),
]


def sum_quarter(parts):
    return pl.pallas_call(
        quarter_kernel,
        out_shape=HALVES,
        in_specs=[MASS] * 4,
        out_specs=[MASS] * 2,
        compiler_params=room(16),
        name="sum_quarter",
    )(*parts)


def pair_kernel(*refs):
    mine, came, outs = refs[:2], refs[2:4], refs[4:]
    for half in range(2):
        total = mine[half][:BLK].astype(jnp.float32) + came[half][:BLK].astype(jnp.float32)
        outs[half][:BLK] = total.astype(jnp.bfloat16)
    put_terms(outs[0], BLK, split_terms(largest([mine[0][BLK:, :BLK], came[0][BLK:, :BLK]])))


def add_pairs(mine, came):
    return pl.pallas_call(
        pair_kernel,
        out_shape=HALVES,
        in_specs=[MASS] * 4,
        out_specs=[MASS] * 2,
        compiler_params=room(16),
        name="add_pairs",
    )(*mine, *came)


def join_kernel(*refs):
    mine, came, outs, peak_ref = refs[:2], refs[2:4], refs[4:6], refs[6]
    for half in range(2):
        total = mine[half][:BLK].astype(jnp.float32) + came[half][:BLK].astype(jnp.float32)
        outs[half][...] = total.astype(jnp.bfloat16)
    peak_ref[...] = largest([mine[0][BLK:, :BLK], came[0][BLK:, :BLK]])


def join_pairs(mine, came):
    return pl.pallas_call(
        join_kernel,
        out_shape=[jax.ShapeDtypeStruct((BLK, BAND), jnp.bfloat16)] * 2
        + [jax.ShapeDtypeStruct((1, BLK), jnp.float32)],
        in_specs=[MASS] * 4,
        out_specs=[MASS] * 3,
        compiler_params=room(16),
        name="join_pairs",
    )(*mine, *came)


def step_kernel(x_ref, *refs):
    pieces = refs[:16]
    outs, (band_ref, gram_ref, first_ref, round_ref) = refs[16 : 16 + NZ], refs[16 + NZ :]
    *places, core = own_place()
    for side in range(2):
        for d in range(4):
            start = quarter_rows(places[side] + (4 - d), side * HALF).start
            for half in range(2):
                rows = pl.ds(pl.multiple_of(start + half * BLK, BLK), BLK)
                band_ref[rows, :] = pieces[side * 8 + d * 2 + half][...]
    for i in range(NB):
        block = band_ref[pl.ds(i * BLK, BLK), :]
        turned = block[:, BLK : BAND - BLK].T
        for d in range(NB // 2 + 1):
            j = (i + d) % NB
            gram_ref[pl.ds(i * BLK, BLK), pl.ds(j * BLK, BLK)] = block[:, d * BLK : (d + 1) * BLK]
            if 1 <= d < NB // 2:
                gram_ref[pl.ds(j * BLK, BLK), pl.ds(i * BLK, BLK)] = turned[(d - 1) * BLK : d * BLK]

    ones = jnp.ones((16, FF), jnp.bfloat16)
    bound = jnp.zeros((1, 1), jnp.float32)
    for n in range(FF // CUT):
        columns = pl.ds(n * CUT, CUT)
        gram = gram_ref[:, columns]
        first_ref[:, columns] = jnp.dot(x_ref[...], gram, preferred_element_type=jnp.float32)
        sums = jnp.dot(ones, jnp.abs(gram), preferred_element_type=jnp.float32)
        bound = jnp.maximum(bound, jnp.max(sums[:8], keepdims=True))
    inverse = 1.0 / bound
    scale = rms_match * math.sqrt(max(D, FF)) / jnp.sqrt(bound)
    for n in range(FF // CUT):
        columns = pl.ds(n * CUT, CUT)
        first = first_ref[:, columns] * inverse
        round_ref[:, columns] = first.astype(jnp.bfloat16)
        first_ref[:, columns] = linear_coef * x_ref[:, columns].astype(jnp.float32) + cubic_coef * first
    for n in range(FF // CUT):
        columns = pl.ds(n * CUT, CUT)
        second = jnp.dot(round_ref[...], gram_ref[:, columns], preferred_element_type=jnp.float32) * inverse
        step = scale * (first_ref[:, columns] + quintic_coef * second)
        step = step.reshape(NZ, PADROWS, CUT)
        head, tail = pack([step[:, 8 * t : 8 * t + 8] for t in range(4)])
        target = (n + 2 * core) % 4
        for d in range(NZ):
            outs[d][:, head_columns(target)] = head[d]
            outs[d][:, tail_columns(target)] = tail[d]


def finish(mine, pieces):
    return pl.pallas_call(
        step_kernel,
        out_shape=[jax.ShapeDtypeStruct((16, PACKED), jnp.bfloat16)] * NZ,
        in_specs=[MASS] * 17,
        out_specs=[MASS] * NZ,
        scratch_shapes=[
            pltpu.VMEM((FF, BAND), jnp.bfloat16),
            pltpu.VMEM((FF, FF), jnp.bfloat16),
            pltpu.VMEM((KROWS, FF), jnp.float32),
            pltpu.VMEM((KROWS, FF), jnp.bfloat16),
        ],
        compiler_params=room(28),
        name="finish",
    )(mine, *pieces)


def clip_kernel(peak_ref, q_ref, k_ref, q_out, k_out):
    z = lax.axis_index("z")
    gamma = jnp.minimum(1.0, clip_limit / peak_ref[...])
    square = (BLK, BLK)
    diagonal = lax.broadcasted_iota(jnp.int32, square, 0) == lax.broadcasted_iota(jnp.int32, square, 1)
    gamma = jnp.sum(jnp.where(diagonal, jnp.broadcast_to(gamma, square), 0.0), axis=1, keepdims=True)
    root = jnp.sqrt(gamma)
    for source, out, width in ((q_ref, q_out, NOPE + ROPE), (k_ref, k_out, NOPE)):
        columns = source.shape[1]
        column = lax.broadcasted_iota(jnp.int32, (BLK, columns), 1)
        head = column // width
        chosen = lax.broadcasted_iota(jnp.int32, (BLK, columns), 0) == head + z * (columns // width)
        value = jnp.where(column - head * width < NOPE, root, gamma)
        factor = jnp.sum(jnp.where(chosen, value, 0.0), axis=0, keepdims=True)
        out[...] = (source[...].astype(jnp.float32) * factor).astype(jnp.bfloat16)


def clip(peak, q_weight, k_weight):
    return pl.pallas_call(
        clip_kernel,
        out_shape=[jax.ShapeDtypeStruct(weight.shape, jnp.bfloat16) for weight in (q_weight, k_weight)],
        in_specs=[MASS] * 3,
        out_specs=[MASS] * 2,
        compiler_params=room(16),
        name="clip",
    )(peak, q_weight, k_weight)


def place_of(x, y, core):
    return (x * NY + y) * NC + core


def permutation(step):
    pairs = []
    for x in range(NX):
        for y in range(NY):
            for core in range(NC):
                mine = (x, y) if core == 0 else (y, x)
                to = step(*mine)
                to = to if core == 0 else to[::-1]
                pairs.append((place_of(x, y, core), place_of(*to, core)))
    return pairs


def send_along(value, by):
    return lax.ppermute(value, PLANE, permutation(lambda along, across: ((along + by) % 4, across)))


LINKS = ((1, 0, 3, 2), (3, 2, 1, 0))


def trade_across(values, first):
    links = (LINKS[first], LINKS[1 - first])
    return [
        lax.ppermute(value, PLANE, permutation(lambda along, across, link=link: (along, link[across])))
        for value, link in zip(values, links)
    ]


def collect(own, sends, order):
    came = {d: send_along(sends(d), d) for d in order}
    return [own, came[1], came[2], came[3]]


def relay(low, high):
    from_before = [send_along(low, 1), None]
    from_behind = [None, send_along(high, 3)]
    from_before[1] = send_along(high, 1)
    from_behind[0] = send_along(low, 3)
    across = [send_along(from_before[0], 1), send_along(from_behind[1], 3)]
    return [low, high] + from_before + across + from_behind


def swap_cores(value):
    return lax.ppermute(value, "c", [(0, 1), (1, 0)])


def trade_planes(blocks, sign):
    came = [blocks[0]] + [None] * (NZ - 1)
    for d in (4, 1, 7, 3, 5, 2, 6):
        came[d] = lax.ppermute(blocks[d], "z", [(i, (i + sign * d) % NZ) for i in range(NZ)])
    return came


def body(grads, momentum, max_logits, q_weight, k_weight):
    grads, momentum = jnp.swapaxes(grads, 0, 1), jnp.swapaxes(momentum, 0, 1)
    max_logits = pltpu.with_memory_space_constraint(max_logits, pltpu.HBM)
    blocks = find_direction(max_logits, grads, momentum)
    owned = trade_planes(blocks, 1)
    other = [None] * NZ
    for d in (0, 4, 3, 5, 2, 6, 1, 7):
        other[d] = swap_cores(owned[d])
    *shares, mine = gram_band(owned + other)
    shares[0], grads_again, momentum = lax.optimization_barrier((shares[0], grads, momentum))
    parts = collect(shares[0], lambda d: shares[d], (1, 3, 2))
    new_momentum = add_momentum(grads_again, momentum)
    parts[0], new_momentum = lax.optimization_barrier((parts[0], new_momentum))
    held = sum_quarter(parts)
    held = add_pairs(held, trade_across(held, 0))
    low, high, peak = join_pairs(held, trade_across(held, 1))
    pieces = relay(low, high)
    q_clipped, k_clipped = clip(peak, q_weight, k_weight)
    pieces[0], pieces[2], q_clipped, k_clipped = lax.optimization_barrier((pieces[0], pieces[2], q_clipped, k_clipped))
    other = [None] * len(pieces)
    for n in (0, 1, 2, 7, 3, 6, 4, 5):
        other[n] = swap_cores(pieces[n])
    step = finish(mine, pieces + other)
    step = trade_planes(step, -1)
    step = jnp.swapaxes(spread_step(step, grads.shape[0]), 0, 1)
    return (jnp.swapaxes(new_momentum, 0, 1), step, q_clipped, k_clipped)


def solution(mesh):
    split = Mesh(mesh.devices.reshape(NX, NY, NC, NZ), ("x", "y", "c", "z"))
    rows = P(None, ("x", "y", "c", "z"), None)
    heads = P(("x", "y", "c"), "z")
    return jax.shard_map(
        body,
        mesh=split,
        in_specs=(rows, rows, P(("x", "y", "c", "z"), None), heads, heads),
        out_specs=(rows, rows, heads, heads),
        check_vma=False,
    )
```
